256 devices in a mesh: probe: 64 (over x, z, y_lo), slab: 4 (over y_hi, core).
Axes of the slice: x: 4, y: 4 (y_hi: 2, y_lo: 2; y = y_hi * 2 + y_lo), z: 8, core: 2. Of those that a mesh axis runs over, the one named last changes fastest.
Arguments:
- incident_prev: float32 [128, 256, 512], P('slab', 'probe'), may hold values from -6 to 6
- incident_now: float32 [128, 256, 512], P('slab', 'probe'), may hold values from -6 to 6
- forcing: float32 [2, 128, 256, 512], P(None, 'slab', 'probe'), may hold values from -4 to 4
- stiffness: float32 [128, 256, 512], P('slab', 'probe'), may hold values from 0.05 to 0.2
- probe_prev: float32 [128, 2048, 512], P('slab', 'probe'), may hold values from -6 to 6
- probe_now: float32 [128, 2048, 512], P('slab', 'probe'), may hold values from -6 to 6
- perturb: float32 [128, 2048, 512], P('slab', 'probe'), may hold values from -4 to 4
Outputs:
- probe_out: float32 [128, 2048, 512], P('slab', 'probe')
- incident_out: float32 [128, 256, 512], P('slab', 'probe')
The draws below stay inside these ranges and needn't reach their ends.
All inputs are finite; a program needn't handle non-finite values.
Results may differ from the reference program's by a relative error of at most 0.00002.
Values sent between devices are 32-bit elements; how exact they have to be, the bound alone decides.
A program may use at most 128 MiB of HBM per device.

```python
import jax
import jax.numpy as jnp
from jax import lax

NX = 512
PROBES_ALL = 8
STEPS = 2
BLOCKS = 8
PROW = 32
NY = 256
NZ = 128


def block_scale(key, shape, split, low, top_value):
    def one(axis_at, shards_of):
        heights = jax.random.uniform(jax.random.fold_in(jax.random.fold_in(key, 6), axis_at), (shards_of,), jnp.float32, low / len(split), top_value / len(split))
        return jnp.repeat(jnp.exp(heights), shape[axis_at] // shards_of).reshape((-1,) + (1,) * (len(shape) - axis_at - 1))

    loudness = one(*split[0])
    for cut in split[1:]:
        loudness = loudness * one(*cut)
    return loudness


def bell_draw(key, shape, scale, most, shards=(), kind=jnp.bfloat16):
    result = jax.random.normal(key, shape, jnp.float32) * scale
    if len(shards) > 0:
        result = block_scale(key, shape, shards, -0.22, 0.18) * result
    return jnp.clip(result, min=-most, max=most).astype(kind)


def setup_inputs(seed: int = 0) -> dict:
    arg_keys = jax.random.split(jax.random.key(seed), 8)
    incident_prev = bell_draw(arg_keys[0], (NZ, NY, NX), 1.0, 6.0, ((0, 4), (1, 64)), jnp.float32)
    incident_now = bell_draw(arg_keys[1], (NZ, NY, NX), 1.0, 6.0, ((0, 4), (1, 64)), jnp.float32)
    forcing = bell_draw(arg_keys[2], (STEPS, NZ, NY, NX), 0.5, 4.0, ((1, 4), (2, 64)), jnp.float32)
    stiffness = jnp.clip(0.05 + 0.15 * jax.random.uniform(arg_keys[3], (NZ, NY, NX), jnp.float32) ** block_scale(arg_keys[3], (NZ, NY, NX), ((0, 4), (1, 64)), -0.2, 0.2), 0.05, 0.2)
    probe_prev = bell_draw(arg_keys[4], (NZ, PROBES_ALL * NY, NX), 1.0, 6.0, ((0, 4), (1, 64)), jnp.float32)
    probe_now = bell_draw(arg_keys[5], (NZ, PROBES_ALL * NY, NX), 1.0, 6.0, ((0, 4), (1, 64)), jnp.float32)
    perturb = bell_draw(arg_keys[6], (NZ, PROBES_ALL * NY, NX), 1.0, 4.0, ((0, 4), (1, 64)), jnp.float32)
    return {"incident_prev": incident_prev, "incident_now": incident_now, "forcing": forcing, "stiffness": stiffness, "probe_prev": probe_prev, "probe_now": probe_now, "perturb": perturb}


stencil_reach = 4
coefficients = (-205.0 / 72.0, 8.0 / 5.0, -1.0 / 5.0, 8.0 / 315.0, -1.0 / 560.0)


def laplace(extended, dims):
    middle = [slice(stencil_reach, size - stencil_reach) if d in dims else slice(None) for d, size in enumerate(extended.shape)]
    summed = coefficients[0] * len(dims) * extended[tuple(middle)]
    for d in dims:
        n = extended.shape[d] - 2 * stencil_reach
        for j in range(1, 5):
            lower_cut = list(middle)
            lower_cut[d] = slice(stencil_reach - j, stencil_reach - j + n)
            upper_cut = list(middle)
            upper_cut[d] = slice(stencil_reach + j, stencil_reach + j + n)
            summed = summed + coefficients[j] * (extended[tuple(lower_cut)] + extended[tuple(upper_cut)])
    return summed


def unfold(packed):
    return jnp.transpose(packed.reshape(NZ, BLOCKS, PROBES_ALL, PROW, NX), (2, 0, 1, 3, 4)).reshape(PROBES_ALL, NZ, NY, NX)


def refold(fields):
    return jnp.transpose(fields.reshape(PROBES_ALL, NZ, BLOCKS, PROW, NX), (1, 2, 0, 3, 4)).reshape(NZ, PROBES_ALL * NY, NX)


def reference(incident_prev, incident_now, forcing, stiffness, probe_prev, probe_now, perturb):
    previous, current = incident_prev, incident_now
    laplacians = []
    for moment in range(STEPS):
        laplacian = laplace(jnp.pad(current, stencil_reach), (0, 1, 2))
        laplacians.append(laplacian)
        previous, current = current, 2.0 * current - previous + stiffness * laplacian + forcing[moment]

    def advance(fields):
        older_field, newer_field, relative = fields
        for moment in range(STEPS):
            probe_lap = laplace(jnp.pad(newer_field, stencil_reach), (0, 1, 2))
            older_field, newer_field = newer_field, 2.0 * newer_field - older_field + stiffness * probe_lap + 2.0 * stiffness * relative * laplacians[moment]
        return newer_field

    probe_out = lax.map(advance, (unfold(probe_prev), unfold(probe_now), unfold(perturb)))
    return refold(probe_out), current
```

```python
import functools

import jax
import jax.numpy as jnp
from jax import lax
from jax.experimental import pallas as pl
from jax.experimental.pallas import tpu as pltpu
from jax.sharding import PartitionSpec as P

coefficients = (-205.0 / 72.0, 8.0 / 5.0, -1.0 / 5.0, 8.0 / 315.0, -1.0 / 560.0)
SCALE = 5040
BAND = (0.0, 8064.0, -1008.0, 128.0, -9.0)

GROUP = 8
REACH = 4
MESH = pl.DeviceIdType.MESH
F32 = jnp.float32


def kernel(
    depth, rows, nx, n_probe, n_slab,
    iprev, inow, forcing, stiff, pprev, pnow, pert,
    probe_out, inc_out,
    U0, U1, UH, IP, FO, YE, XS, G, E0, E1, PP, PT, L, SB, DH, CL, B,
    ssG, rsG, ssU, rsU, ssD, rsD, ls,
):
    Pi = lax.axis_index("probe")
    Si = lax.axis_index("slab")
    p = Pi % GROUP
    zl = p // 2
    yl = p % 2
    z1 = zl + 1 - 2 * (zl % 2)
    z2 = (zl + 2) % 4
    z3 = 3 - zl
    base = Pi - p
    inner = jnp.logical_or(zl == 1, zl == 2)
    partner = Pi + 1 - 2 * yl
    own = rows // GROUP

    def zdev(k):
        return (base + (z1, z2, z3)[k] * 2 + yl, Si)

    def zslot(k):
        return (z1, z2, z3)[k] * 2 + yl

    has_p_lo, has_p_hi = Pi > 0, Pi < n_probe - 1
    has_b_lo, has_b_hi = Pi >= GROUP, Pi < n_probe - GROUP
    has_s_lo, has_s_hi = Si > 0, Si < n_slab - 1

    loads = [
        pltpu.make_async_copy(inow, U0.at[pl.ds(REACH, depth)], ls.at[0]),
        pltpu.make_async_copy(stiff, G.at[0, p], ls.at[1]),
        pltpu.make_async_copy(pnow, E0.at[pl.ds(REACH, depth), pl.ds(8, rows)], ls.at[2]),
        pltpu.make_async_copy(iprev, IP, ls.at[3]),
        pltpu.make_async_copy(forcing, FO, ls.at[4]),
        pltpu.make_async_copy(pprev, PP, ls.at[5]),
        pltpu.make_async_copy(pert, PT, ls.at[6]),
    ]
    for c in loads:
        c.start()

    bar = pltpu.get_barrier_semaphore()

    def hello(dev):
        pl.semaphore_signal(bar, inc=1, device_id=dev, device_id_type=MESH)

    for k in range(3):
        hello(zdev(k))
    hello((partner, Si))
    sides = [
        (has_p_lo, (Pi - 1, Si)), (has_p_hi, (Pi + 1, Si)),
        (has_b_lo, (Pi - GROUP, Si)), (has_b_hi, (Pi + GROUP, Si)),
        (has_s_lo, (Pi, Si - 1)), (has_s_hi, (Pi, Si + 1)),
    ]
    for cond, dev in sides:
        pl.when(cond)(functools.partial(hello, dev))
    peers = 4
    for cond, _ in sides:
        peers = peers + cond.astype(jnp.int32)
    pl.semaphore_wait(bar, peers)

    def remote(src, dst, ssem, rsem, dev):
        return pltpu.make_async_remote_copy(
            src_ref=src, dst_ref=dst, send_sem=ssem, recv_sem=rsem,
            device_id=dev, device_id_type=MESH,
        )

    pending = []

    def send(cond, desc):
        if cond is None:
            desc.start()
        else:
            pl.when(cond)(desc.start)
        pending.append((cond, desc))

    def rims_incident(step, src, U):
        send(has_p_lo, remote(src, UH.at[step, 1], ssU.at[step, 0], rsU.at[step, 1], (Pi - 1, Si)))
        send(has_p_hi, remote(src, UH.at[step, 0], ssU.at[step, 1], rsU.at[step, 0], (Pi + 1, Si)))
        send(has_s_lo, remote(src.at[pl.ds(0, REACH)], U.at[pl.ds(depth + REACH, REACH)],
                              ssU.at[step, 2], rsU.at[step, 3], (Pi, Si - 1)))
        send(has_s_hi, remote(src.at[pl.ds(depth - REACH, REACH)], U.at[pl.ds(0, REACH)],
                              ssU.at[step, 3], rsU.at[step, 2], (Pi, Si + 1)))

    def wait_incident(step, U):
        for side, cond in ((0, has_p_lo), (1, has_p_hi)):
            d = remote(UH.at[step, side], UH.at[step, side], ssU.at[step, side], rsU.at[step, side], (partner, Si))
            pl.when(cond)(d.wait_recv)
        for side, cond, at in ((2, has_s_lo, 0), (3, has_s_hi, depth + REACH)):
            r = U.at[pl.ds(at, REACH)]
            d = remote(r, r, ssU.at[step, side], rsU.at[step, side], (partner, Si))
            pl.when(cond)(d.wait_recv)

    def send_depth(step, low, high, E):
        send(has_s_lo, remote(low, E.at[pl.ds(depth + REACH, REACH), pl.ds(8, rows)],
                              ssD.at[step, 2], rsD.at[step, 3], (Pi, Si - 1)))
        send(has_s_hi, remote(high, E.at[pl.ds(0, REACH), pl.ds(8, rows)],
                              ssD.at[step, 3], rsD.at[step, 2], (Pi, Si + 1)))

    def wait_depth(step, E):
        for side, cond, at in ((2, has_s_lo, 0), (3, has_s_hi, depth + REACH)):
            r = E.at[pl.ds(at, REACH), pl.ds(8, rows)]
            d = remote(r, r, ssD.at[step, side], rsD.at[step, side], (partner, Si))
            pl.when(cond)(d.wait_recv)

    def send_rim(step, side):
        if side == 0:
            send(has_b_lo, remote(SB.at[step, 0], DH.at[step, 1], ssD.at[step, 0], rsD.at[step, 1], (Pi - GROUP, Si)))
        else:
            send(has_b_hi, remote(SB.at[step, 1], DH.at[step, 0], ssD.at[step, 1], rsD.at[step, 0], (Pi + GROUP, Si)))

    def wait_rim(step, side):
        r = DH.at[step, side]
        d = remote(r, r, ssD.at[step, side], rsD.at[step, side], (partner, Si))
        pl.when((has_b_lo, has_b_hi)[side])(d.wait_recv)

    def gather_own(a, src):
        dst = G.at[a, p]
        send(None, remote(src, dst, ssG.at[a, 1], rsG.at[a, p], zdev(0)))
        send(None, remote(src, dst, ssG.at[a, 2], rsG.at[a, p], zdev(1)))
        send(inner, remote(src, dst, ssG.at[a, 3], rsG.at[a, p], zdev(2)))
        send(None, remote(src, dst, ssG.at[a, 0], rsG.at[a, p], (partner, Si)))

    def gather_forward(a):
        for k in range(3):
            slot = zslot(k)
            r = G.at[a, slot]
            remote(r, r, ssG.at[a, 4 + k], rsG.at[a, slot], (partner, Si)).wait_recv()
            if k == 1:
                send(inner, remote(r, r, ssG.at[a, 7], rsG.at[a, slot], zdev(0)))
            send(None, remote(r, r, ssG.at[a, 4 + k], rsG.at[a, slot], (partner, Si)))

    def gather_wait(a, q):
        r = G.at[a, q]
        d = remote(r, r, ssG.at[a, 0], rsG.at[a, q], (partner, Si))
        pl.when((q % 2) != yl)(d.wait_recv)

    rims_incident(0, inow, U0)
    gather_own(0, stiff)
    send_depth(0, pnow.at[pl.ds(0, REACH)], pnow.at[pl.ds(depth - REACH, REACH)], E0)

    loads[2].wait()

    def pack(z, _):
        SB[0, 0, z] = E0[z + REACH, 8:12, :]
        SB[0, 1, z] = E0[z + REACH, rows + 4:rows + 8, :]
        return 0

    lax.fori_loop(0, depth, pack, 0)
    send_rim(0, 0)
    send_rim(0, 1)

    def band(i, _):
        r = lax.broadcasted_iota(jnp.int32, (64, nx), 0) + i * 64
        c = lax.broadcasted_iota(jnp.int32, (64, nx), 1)
        gap = jnp.abs(r - c)
        v = jnp.zeros((64, nx), F32)
        for j in range(1, 5):
            v = jnp.where(gap == j, BAND[j], v)
        B[pl.ds(pl.multiple_of(i * 64, 64), 64), :] = v.astype(jnp.bfloat16)
        return 0

    lax.fori_loop(0, nx // 64, band, 0)

    edge = jnp.zeros((8, nx), F32)

    def clear(z, _):
        for E in (E0, E1):
            E[z + REACH, 0:8, :] = edge
            E[z + REACH, rows + 8:rows + 16, :] = edge
        CL[z, 0, :, :] = edge
        CL[z, 1, :, :] = edge
        return 0

    lax.fori_loop(0, depth, clear, 0)
    for cond, at in ((has_s_lo, 0), (has_s_hi, depth + REACH)):

        @pl.when(jnp.logical_not(cond))
        def _(at=at):
            for i in range(REACH):
                for E in (E0, E1):
                    E[at + i, 8:8 + rows, :] = jnp.zeros((rows, nx), F32)
                for U in (U0, U1):
                    U[at + i] = jnp.zeros((own, nx), F32)

    for side, cp, cb in ((0, has_p_lo, has_b_lo), (1, has_p_hi, has_b_hi)):
        for R, cond in ((UH, cp), (DH, cb)):

            @pl.when(jnp.logical_not(cond))
            def _(R=R, side=side):
                def zero(z, _):
                    for step in range(2):
                        R[step, side, z] = jnp.zeros((own, nx), F32)
                    return 0

                lax.fori_loop(0, depth, zero, 0)

    def along_x(D):
        hi = D.astype(jnp.bfloat16)
        lo = (D - hi.astype(F32)).astype(jnp.bfloat16)
        X = jnp.dot(hi, B[...], preferred_element_type=F32)
        X = X + jnp.dot(lo, B[...], preferred_element_type=F32)
        return X * (1.0 / SCALE)

    def incident(step, U, older, into):
        def build(z, _):
            YE[z, 4:8, :] = UH[step, 0, z]
            YE[z, 8:12, :] = U[z + REACH]
            YE[z, 12:16, :] = UH[step, 1, z]
            return 0

        lax.fori_loop(0, depth, build, 0)
        XS[...] = along_x(YE[:, 8:16, :].reshape(depth * 8, nx)).reshape(depth, 8, nx)

        def point(z, _):
            c = U[z + REACH]
            acc = XS[z, 0:4, :] + (3.0 * coefficients[0]) * c
            for j in range(1, 5):
                acc = acc + coefficients[j] * (U[z + REACH - j] + U[z + REACH + j])
            for j in range(1, 5):
                acc = acc + coefficients[j] * (YE[z, 8 - j:12 - j, :] + YE[z, 8 + j:12 + j, :])
            G[1 + step, p, z] = acc
            into(z, 2.0 * c - older(z) + G[0, p, z] * acc + FO[step, z])
            return 0

        lax.fori_loop(0, depth, point, 0)

    def laplace(E):
        def wide(c, _):
            z0 = c * 8
            D = E[pl.ds(z0 + REACH, 8), 8:8 + rows, :].reshape(8 * rows, nx)
            L[pl.ds(z0, 8)] = along_x(D).reshape(8, rows, nx)
            return 0

        lax.fori_loop(0, depth // 8, wide, 0)

        def point(z, _):
            acc = L[z] + (3.0 * coefficients[0]) * E[z + REACH, 8:8 + rows, :]
            for j in range(1, 5):
                acc = acc + coefficients[j] * (E[z + REACH - j, 8:8 + rows, :] + E[z + REACH + j, 8:8 + rows, :])
            for j in range(1, 5):
                acc = acc + coefficients[j] * (
                    E[z + REACH, 8 - j:8 - j + rows, :] + E[z + REACH, 8 + j:8 + j + rows, :]
                )
            L[z] = acc
            return 0

        lax.fori_loop(0, depth, point, 0)

    def update(step, q, newer, older, into):
        gather_wait(0, q) if step == 0 else None
        gather_wait(1 + step, q)
        side = 0 if q == 0 else 1 if q == GROUP - 1 else None
        if side is not None:
            wait_rim(step, side)
        at = q * own

        def point(z, _):
            lap = L[z, at:at + own, :]
            if side == 0:
                CL[z, 0, 0:4, :] = DH[step, 0, z]
                for j in range(1, 5):
                    lap = lap + coefficients[j] * CL[z, 0, 4 - j:8 - j, :]
            if side == 1:
                CL[z, 1, 4:8, :] = DH[step, 1, z]
                for j in range(1, 5):
                    lap = lap + coefficients[j] * CL[z, 1, j:j + 4, :]
            value = (
                2.0 * newer(z, at) - older(z, at)
                + G[0, q, z] * (lap + 2.0 * PT[z, at:at + own, :] * G[1 + step, q, z])
            )
            into(z, at, value)
            if step == 0 and side is not None:
                SB[1, side, z] = value
            return 0

        lax.fori_loop(0, depth, point, 0)

    for i in (0, 1, 3, 4):
        loads[i].wait()
    wait_incident(0, U0)

    def into_u1(z, v):
        U1[z + REACH] = v

    incident(0, U0, lambda z: IP[z], into_u1)
    rims_incident(1, U1.at[pl.ds(REACH, depth)], U1)
    gather_own(1, G.at[1, p])

    gather_forward(0)
    wait_depth(0, E0)
    laplace(E0)

    wait_incident(1, U1)

    def into_out(z, v):
        inc_out[z] = v

    incident(1, U1, lambda z: U0[z + REACH], into_out)
    gather_own(2, G.at[2, p])
    gather_forward(1)

    loads[5].wait()
    loads[6].wait()

    def into_e1(z, at, v):
        E1[z + REACH, 8 + at:8 + at + own, :] = v

    def from_e(E):
        return lambda z, at: E[z + REACH, 8 + at:8 + at + own, :]

    for q in (0, GROUP - 1) + tuple(range(1, GROUP - 1)):
        update(0, q, from_e(E0), lambda z, at: PP[z, at:at + own, :], into_e1)
        if q == 0:
            send_rim(1, 0)
        if q == GROUP - 1:
            send_rim(1, 1)
    send_depth(1, E1.at[pl.ds(REACH, REACH), pl.ds(8, rows)], E1.at[pl.ds(depth, REACH), pl.ds(8, rows)], E1)

    gather_forward(2)
    wait_depth(1, E1)
    laplace(E1)

    def into_probe(z, at, v):
        probe_out[z, at:at + own, :] = v

    for q in tuple(range(1, GROUP - 1)) + (0, GROUP - 1):
        update(1, q, from_e(E1), from_e(E0), into_probe)

    for cond, d in pending:
        if cond is None:
            d.wait_send()
        else:
            pl.when(cond)(d.wait_send)


def local(n_probe, n_slab, iprev, inow, forcing, stiff, pprev, pnow, pert):
    depth, own, nx = inow.shape
    rows = pnow.shape[1]
    dma = pltpu.SemaphoreType.DMA
    vm = pltpu.VMEM
    return pl.pallas_call(
        functools.partial(kernel, depth, rows, nx, n_probe, n_slab),
        out_shape=(
            jax.ShapeDtypeStruct(pnow.shape, F32),
            jax.ShapeDtypeStruct(inow.shape, F32),
        ),
        in_specs=[pl.BlockSpec(memory_space=pl.ANY)] * 7,
        out_specs=(pl.BlockSpec(memory_space=pltpu.VMEM), pl.BlockSpec(memory_space=pltpu.VMEM)),
        scratch_shapes=[
            vm((depth + 8, own, nx), F32),
            vm((depth + 8, own, nx), F32),
            vm((2, 2, depth, own, nx), F32),
            vm((depth, own, nx), F32),
            vm((2, depth, own, nx), F32),
            vm((depth, 16, nx), F32),
            vm((depth, 8, nx), F32),
            vm((3, GROUP, depth, own, nx), F32),
            vm((depth + 8, rows + 16, nx), F32),
            vm((depth + 8, rows + 16, nx), F32),
            vm((depth, rows, nx), F32),
            vm((depth, rows, nx), F32),
            vm((depth, rows, nx), F32),
            vm((2, 2, depth, own, nx), F32),
            vm((2, 2, depth, own, nx), F32),
            vm((depth, 2, 8, nx), F32),
            vm((nx, nx), jnp.bfloat16),
            dma((3, 8)), dma((3, 8)), dma((2, 4)), dma((2, 4)), dma((2, 4)), dma((2, 4)), dma((7,)),
        ],
        compiler_params=pltpu.CompilerParams(
            collective_id=0, has_side_effects=True, vmem_limit_bytes=56 * 1024 * 1024
        ),
        name="born",
    )(iprev, inow, forcing, stiff, pprev, pnow, pert)


def solution(mesh):
    spec = P("slab", "probe", None)
    return jax.shard_map(
        functools.partial(local, mesh.shape["probe"], mesh.shape["slab"]),
        mesh=mesh,
        in_specs=(spec, spec, P(None, "slab", "probe", None), spec, spec, spec, spec),
        out_specs=(spec, spec),
        check_vma=False,
    )
```

```python
import functools

import jax
import jax.numpy as jnp
from jax import lax
from jax.experimental import pallas as pl
from jax.experimental.pallas import tpu as pltpu
from jax.sharding import PartitionSpec as P

coefficients = (-205.0 / 72.0, 8.0 / 5.0, -1.0 / 5.0, 8.0 / 315.0, -1.0 / 560.0)
SCALE = 5040
BAND = (0.0, 8064.0, -1008.0, 128.0, -9.0)

GROUP = 8
REACH = 4
MESH = pl.DeviceIdType.MESH
RELAYED = (False, False)
ORDER = (
    "rims_u0", "own_s", "depth_0", "pack", "constants", "incident_0", "rims_u1", "own_0", "fwd_s0", "fwd_s1", "rims_0", "fwd_s2", "pass_0", "hear_0", "lap_00", "lap_01", "incident_1", "own_1", "fwd_00", "fwd_01", "fwd_02", "loads", "new_00", "new_07", "new_01", "new_02", "new_03", "new_04", "new_05", "new_06", "depth_1", "fwd_10", "fwd_11", "rims_1", "hear_1", "lap_10", "lap_11", "fwd_12", "pass_1", "new_11", "new_12", "new_13", "new_14", "new_15", "new_16", "new_10", "new_17",
)
F32 = jnp.float32


def kernel(
    depth, rows, nx, n_probe, n_slab,
    iprev, inow, forcing, stiff, pprev, pnow, pert,
    probe_out, inc_out,
    U0, U1, UH, IP, FO, YE, XS, G, E0, E1, PP, PT, L, SB, DH, RX, CL, B,
    ssG, rsG, ssU, rsU, ssD, rsD, ls,
):
    Pi = lax.axis_index("probe")
    Si = lax.axis_index("slab")
    p = Pi % GROUP
    zl = p // 2
    yl = p % 2
    z1 = zl + 1 - 2 * (zl % 2)
    z2 = (zl + 2) % 4
    z3 = 3 - zl
    base = Pi - p
    inner = jnp.logical_or(zl == 1, zl == 2)
    partner = Pi + 1 - 2 * yl
    own = rows // GROUP

    def zdev(k):
        return (base + (z1, z2, z3)[k] * 2 + yl, Si)

    def zslot(k):
        return (z1, z2, z3)[k] * 2 + yl

    has_p_lo, has_p_hi = Pi > 0, Pi < n_probe - 1
    has_b_lo, has_b_hi = Pi >= GROUP, Pi < n_probe - GROUP
    has_s_lo, has_s_hi = Si > 0, Si < n_slab - 1
    block, last = Pi // GROUP, n_probe // GROUP - 1
    from_lo, relay_lo, to_lo = block == 2, block == 0, block == 1
    from_hi, relay_hi, to_hi = block == last - 2, block == last, block == last - 1

    loads = [
        pltpu.make_async_copy(inow, U0.at[pl.ds(REACH, depth)], ls.at[0]),
        pltpu.make_async_copy(stiff, G.at[0, p], ls.at[1]),
        pltpu.make_async_copy(pnow, E0.at[pl.ds(REACH, depth), pl.ds(8, rows)], ls.at[2]),
        pltpu.make_async_copy(iprev, IP, ls.at[3]),
        pltpu.make_async_copy(forcing, FO, ls.at[4]),
        pltpu.make_async_copy(pprev, PP, ls.at[5]),
        pltpu.make_async_copy(pert, PT, ls.at[6]),
    ]
    for c in loads:
        c.start()

    bar = pltpu.get_barrier_semaphore()

    def hello(dev):
        pl.semaphore_signal(bar, inc=1, device_id=dev, device_id_type=MESH)

    for k in range(3):
        hello(zdev(k))
    hello((partner, Si))
    sides = [
        (has_p_lo, (Pi - 1, Si)), (has_p_hi, (Pi + 1, Si)),
        (has_b_lo, (Pi - GROUP, Si)), (has_b_hi, (Pi + GROUP, Si)),
        (has_s_lo, (Pi, Si - 1)), (has_s_hi, (Pi, Si + 1)),
        (Pi > 1, (Pi - 2, Si)), (Pi < n_probe - 2, (Pi + 2, Si)),
        (jnp.logical_or(from_lo, relay_hi), (Pi - 2 * GROUP, Si)),
        (jnp.logical_or(from_hi, relay_lo), (Pi + 2 * GROUP, Si)),
    ]
    for cond, dev in sides:
        pl.when(cond)(functools.partial(hello, dev))
    peers = 4
    for cond, _ in sides:
        peers = peers + cond.astype(jnp.int32)
    pl.semaphore_wait(bar, peers)

    def remote(src, dst, ssem, rsem, dev):
        return pltpu.make_async_remote_copy(
            src_ref=src, dst_ref=dst, send_sem=ssem, recv_sem=rsem,
            device_id=dev, device_id_type=MESH,
        )

    pending = []

    def send(cond, desc):
        if cond is None:
            desc.start()
        else:
            pl.when(cond)(desc.start)
        pending.append((cond, desc))

    half = depth // 2
    near, far = pl.ds(0, half), pl.ds(half, half)
    lower, upper = yl == 0, yl == 1

    def rims_incident(step, src, U):
        def to(cond, dev, side, part, k):
            send(cond, remote(src.at[part], UH.at[step, side, part], ssU.at[step, k], rsU.at[step, side, k % 2], dev))

        for part, k in ((near, 0), (far, 1)):
            to(lower, (partner, Si), 0, part, k)
            to(upper, (partner, Si), 1, part, k)
        send(has_s_lo, remote(src.at[pl.ds(0, REACH)], U.at[pl.ds(depth + REACH, REACH)],
                              ssU.at[step, 4], rsU.at[step, 3, 0], (Pi, Si - 1)))
        send(has_s_hi, remote(src.at[pl.ds(depth - REACH, REACH)], U.at[pl.ds(0, REACH)],
                              ssU.at[step, 5], rsU.at[step, 2, 0], (Pi, Si + 1)))
        for part, k in ((near, 2), (far, 3))[:1 if RELAYED[step] else 2]:
            to(jnp.logical_and(lower, has_p_lo), (Pi - 1, Si), 1, part, k)
            to(jnp.logical_and(upper, has_p_hi), (Pi + 1, Si), 0, part, k)

    def arrived(step, side, k):
        r = UH.at[step, side, (near, far)[k]]
        remote(r, r, ssU.at[step, 3], rsU.at[step, side, k], (partner, Si)).wait_recv()

    def pass_incident(step):
        for mine, there, side, dev in (
            (lower, Pi < n_probe - 2, 1, (Pi + 2, Si)),
            (upper, Pi > 1, 0, (Pi - 2, Si)),
        ):

            @pl.when(mine)
            def _(side=side):
                arrived(step, side, 1)

            send(jnp.logical_and(mine, there),
                 remote(UH.at[step, side, far], UH.at[step, 1 - side, far], ssU.at[step, 3],
                        rsU.at[step, 1 - side, 1], dev))

    def wait_incident(step, U):
        for mine, side, there in ((lower, 1, has_p_lo), (upper, 0, has_p_hi)):

            @pl.when(mine)
            def _(side=side):
                arrived(step, side, 0)
                if not RELAYED[step]:
                    arrived(step, side, 1)

            @pl.when(jnp.logical_and(mine, there))
            def _(side=side):
                arrived(step, 1 - side, 0)
                arrived(step, 1 - side, 1)

        for side, cond, at in ((2, has_s_lo, 0), (3, has_s_hi, depth + REACH)):
            r = U.at[pl.ds(at, REACH)]
            d = remote(r, r, ssU.at[step, 3], rsU.at[step, side, 0], (partner, Si))
            pl.when(cond)(d.wait_recv)

    def send_depth(step, low, high, E):
        send(has_s_lo, remote(low, E.at[pl.ds(depth + REACH, REACH), pl.ds(8, rows)],
                              ssD.at[step, 2, 0], rsD.at[step, 3, 0], (Pi, Si - 1)))
        send(has_s_hi, remote(high, E.at[pl.ds(0, REACH), pl.ds(8, rows)],
                              ssD.at[step, 3, 0], rsD.at[step, 2, 0], (Pi, Si + 1)))

    def wait_depth(step, E):
        for side, cond, at in ((2, has_s_lo, 0), (3, has_s_hi, depth + REACH)):
            r = E.at[pl.ds(at, REACH), pl.ds(8, rows)]
            d = remote(r, r, ssD.at[step, side, 0], rsD.at[step, side, 0], (partner, Si))
            pl.when(cond)(d.wait_recv)

    def send_rim(step, side):
        cond, by_x, shift, hop = (
            (has_b_lo, from_lo, -GROUP, -2 * GROUP), (has_b_hi, from_hi, GROUP, 2 * GROUP)
        )[side]

        def to(cond, dst, part, k, rsem, dev):
            send(cond, remote(SB.at[step, side, part], dst, ssD.at[step, side, k], rsem, dev))

        out = DH.at[step, 1 - side]
        to(cond, out.at[near], near, 0, rsD.at[step, 1 - side, 0], (Pi + shift, Si))
        to(jnp.logical_and(cond, jnp.logical_not(by_x)), out.at[far], far, 1,
           rsD.at[step, 1 - side, 1], (Pi + shift, Si))
        to(by_x, RX.at[step], far, 2, rsD.at[step, 2, 1], (Pi + hop, Si))

    def pass_rim(step):
        for cond, side, shift in ((relay_lo, 1, GROUP), (relay_hi, 0, -GROUP)):

            @pl.when(cond)
            def _():
                remote(RX.at[step], RX.at[step], ssD.at[step, 3, 1], rsD.at[step, 2, 1], (partner, Si)).wait_recv()

            send(cond, remote(RX.at[step], DH.at[step, side, far], ssD.at[step, 2, 1], rsD.at[step, side, 1],
                              (Pi + shift, Si)))

    def wait_rim(step, side):
        for part, k in ((near, 0), (far, 1)):
            r = DH.at[step, side, part]
            d = remote(r, r, ssD.at[step, side, k], rsD.at[step, side, k], (partner, Si))
            pl.when((has_b_lo, has_b_hi)[side])(d.wait_recv)

    def gather_own(a, src):
        dst = G.at[a, p]
        send(None, remote(src, dst, ssG.at[a, 1], rsG.at[a, p], zdev(0)))
        send(None, remote(src, dst, ssG.at[a, 2], rsG.at[a, p], zdev(1)))
        send(inner, remote(src, dst, ssG.at[a, 3], rsG.at[a, p], zdev(2)))
        send(None, remote(src, dst, ssG.at[a, 0], rsG.at[a, p], (partner, Si)))

    def forward(a, k):
        slot = zslot(k)
        r = G.at[a, slot]
        remote(r, r, ssG.at[a, 4 + k], rsG.at[a, slot], (partner, Si)).wait_recv()
        if k == 1:
            send(inner, remote(r, r, ssG.at[a, 7], rsG.at[a, slot], zdev(0)))
        send(None, remote(r, r, ssG.at[a, 4 + k], rsG.at[a, slot], (partner, Si)))

    def gather_wait(a, q):
        r = G.at[a, q]
        d = remote(r, r, ssG.at[a, 0], rsG.at[a, q], (partner, Si))
        pl.when((q % 2) != yl)(d.wait_recv)

    def pack():
        loads[2].wait()

        def row(z, _):
            SB[0, 0, z] = E0[z + REACH, 8:12, :]
            SB[0, 1, z] = E0[z + REACH, rows + 4:rows + 8, :]
            return 0

        lax.fori_loop(0, depth, row, 0)

    def constants():
        def band(i, _):
            r = lax.broadcasted_iota(jnp.int32, (64, nx), 0) + i * 64
            c = lax.broadcasted_iota(jnp.int32, (64, nx), 1)
            gap = jnp.abs(r - c)
            v = jnp.zeros((64, nx), F32)
            for j in range(1, 5):
                v = jnp.where(gap == j, BAND[j], v)
            B[pl.ds(pl.multiple_of(i * 64, 64), 64), :] = v.astype(jnp.bfloat16)
            return 0

        lax.fori_loop(0, nx // 64, band, 0)

        edge = jnp.zeros((8, nx), F32)

        def clear(z, _):
            for E in (E0, E1):
                E[z + REACH, 0:8, :] = edge
                E[z + REACH, rows + 8:rows + 16, :] = edge
            CL[z, 0, :, :] = edge
            CL[z, 1, :, :] = edge
            return 0

        lax.fori_loop(0, depth, clear, 0)
        for cond, at in ((has_s_lo, 0), (has_s_hi, depth + REACH)):

            @pl.when(jnp.logical_not(cond))
            def _(at=at):
                for i in range(REACH):
                    for E in (E0, E1):
                        E[at + i, 8:8 + rows, :] = jnp.zeros((rows, nx), F32)
                    for U in (U0, U1):
                        U[at + i] = jnp.zeros((own, nx), F32)

        for side, cp, cb in ((0, has_p_lo, has_b_lo), (1, has_p_hi, has_b_hi)):
            for R, cond in ((UH, cp), (DH, cb)):

                @pl.when(jnp.logical_not(cond))
                def _(R=R, side=side):
                    def zero(z, _):
                        for step in range(2):
                            R[step, side, z] = jnp.zeros((own, nx), F32)
                        return 0

                    lax.fori_loop(0, depth, zero, 0)

    def along_x(D):
        hi = D.astype(jnp.bfloat16)
        lo = (D - hi.astype(F32)).astype(jnp.bfloat16)
        X = jnp.dot(hi, B[...], preferred_element_type=F32)
        X = X + jnp.dot(lo, B[...], preferred_element_type=F32)
        return X * (1.0 / SCALE)

    def incident(step, U, older, into):
        def build(z, _):
            YE[z, 4:8, :] = UH[step, 0, z]
            YE[z, 8:12, :] = U[z + REACH]
            YE[z, 12:16, :] = UH[step, 1, z]
            return 0

        lax.fori_loop(0, depth, build, 0)
        XS[...] = along_x(YE[:, 8:16, :].reshape(depth * 8, nx)).reshape(depth, 8, nx)

        def point(z, _):
            c = U[z + REACH]
            acc = XS[z, 0:4, :] + (3.0 * coefficients[0]) * c
            for j in range(1, 5):
                acc = acc + coefficients[j] * (U[z + REACH - j] + U[z + REACH + j])
            for j in range(1, 5):
                acc = acc + coefficients[j] * (YE[z, 8 - j:12 - j, :] + YE[z, 8 + j:12 + j, :])
            G[1 + step, p, z] = acc
            into(z, 2.0 * c - older(z) + G[0, p, z] * acc + FO[step, z])
            return 0

        lax.fori_loop(0, depth, point, 0)

    def laplace(E, part, parts):
        first, end = part * depth // parts, (part + 1) * depth // parts

        def wide(c, _):
            z0 = c * 8
            D = E[pl.ds(z0 + REACH, 8), 8:8 + rows, :].reshape(8 * rows, nx)
            L[pl.ds(z0, 8)] = along_x(D).reshape(8, rows, nx)
            return 0

        lax.fori_loop(first // 8, end // 8, wide, 0)

        def point(z, _):
            acc = L[z] + (3.0 * coefficients[0]) * E[z + REACH, 8:8 + rows, :]
            for j in range(1, 5):
                acc = acc + coefficients[j] * (E[z + REACH - j, 8:8 + rows, :] + E[z + REACH + j, 8:8 + rows, :])
            for j in range(1, 5):
                acc = acc + coefficients[j] * (
                    E[z + REACH, 8 - j:8 - j + rows, :] + E[z + REACH, 8 + j:8 + j + rows, :]
                )
            L[z] = acc
            return 0

        lax.fori_loop(first, end, point, 0)

    def update(step, q, newer, older, into):
        gather_wait(0, q) if step == 0 else None
        gather_wait(1 + step, q)
        side = 0 if q == 0 else 1 if q == GROUP - 1 else None
        if side is not None:
            wait_rim(step, side)
        at = q * own

        def point(z, _):
            lap = L[z, at:at + own, :]
            if side == 0:
                CL[z, 0, 0:4, :] = DH[step, 0, z]
                for j in range(1, 5):
                    lap = lap + coefficients[j] * CL[z, 0, 4 - j:8 - j, :]
            if side == 1:
                CL[z, 1, 4:8, :] = DH[step, 1, z]
                for j in range(1, 5):
                    lap = lap + coefficients[j] * CL[z, 1, j:j + 4, :]
            value = (
                2.0 * newer(z, at) - older(z, at)
                + G[0, q, z] * (lap + 2.0 * PT[z, at:at + own, :] * G[1 + step, q, z])
            )
            into(z, at, value)
            if step == 0 and side is not None:
                SB[1, side, z] = value
            return 0

        lax.fori_loop(0, depth, point, 0, unroll=4)

    def into_u1(z, v):
        U1[z + REACH] = v

    def into_out(z, v):
        inc_out[z] = v

    def into_e1(z, at, v):
        E1[z + REACH, 8 + at:8 + at + own, :] = v

    def into_probe(z, at, v):
        probe_out[z, at:at + own, :] = v

    def from_e(E):
        return lambda z, at: E[z + REACH, 8 + at:8 + at + own, :]

    def incident_0():
        for i in (0, 1, 3, 4):
            loads[i].wait()
        wait_incident(0, U0)
        incident(0, U0, lambda z: IP[z], into_u1)

    def incident_1():
        wait_incident(1, U1)
        incident(1, U1, lambda z: U0[z + REACH], into_out)

    def update_0(q):
        update(0, q, from_e(E0), lambda z, at: PP[z, at:at + own, :], into_e1)

    def update_1(q):
        update(1, q, from_e(E1), from_e(E0), into_probe)

    low, high = pl.ds(REACH, REACH), pl.ds(depth, REACH)
    tasks = {
        "rims_u0": lambda: rims_incident(0, inow, U0),
        "rims_u1": lambda: rims_incident(1, U1.at[pl.ds(REACH, depth)], U1),
        "pass_u0": lambda: pass_incident(0),
        "pass_u1": lambda: pass_incident(1),
        "own_s": lambda: gather_own(0, stiff),
        "own_0": lambda: gather_own(1, G.at[1, p]),
        "own_1": lambda: gather_own(2, G.at[2, p]),
        "depth_0": lambda: send_depth(0, pnow.at[pl.ds(0, REACH)], pnow.at[pl.ds(depth - REACH, REACH)], E0),
        "depth_1": lambda: send_depth(1, E1.at[low, pl.ds(8, rows)], E1.at[high, pl.ds(8, rows)], E1),
        "pack": pack,
        "constants": constants,
        "rims_0": lambda: (send_rim(0, 0), send_rim(0, 1)),
        "rims_1": lambda: (send_rim(1, 0), send_rim(1, 1)),
        "pass_0": lambda: pass_rim(0),
        "pass_1": lambda: pass_rim(1),
        "incident_0": incident_0,
        "incident_1": incident_1,
        "hear_0": lambda: wait_depth(0, E0),
        "hear_1": lambda: wait_depth(1, E1),
        "loads": lambda: (loads[5].wait(), loads[6].wait()),
    }
    for k in range(3):
        for a, name in enumerate("s01"):
            tasks["fwd_%s%d" % (name, k)] = functools.partial(forward, a, k)
    for part in range(2):
        tasks["lap_0%d" % part] = functools.partial(laplace, E0, part, 2)
        tasks["lap_1%d" % part] = functools.partial(laplace, E1, part, 2)
    for q in range(GROUP):
        tasks["new_0%d" % q] = functools.partial(update_0, q)
        tasks["new_1%d" % q] = functools.partial(update_1, q)
    for name in ORDER:
        tasks[name]()

    for cond, d in pending:
        if cond is None:
            d.wait_send()
        else:
            pl.when(cond)(d.wait_send)


def local(n_probe, n_slab, iprev, inow, forcing, stiff, pprev, pnow, pert):
    depth, own, nx = inow.shape
    rows = pnow.shape[1]
    dma = pltpu.SemaphoreType.DMA
    vm = pltpu.VMEM
    return fresh(*pl.pallas_call(
        functools.partial(kernel, depth, rows, nx, n_probe, n_slab),
        out_shape=(pltpu.VMEM(pnow.shape, F32), pltpu.VMEM(inow.shape, F32)),
        in_specs=[pl.BlockSpec(memory_space=pltpu.HBM)] * 7,
        out_specs=(pl.BlockSpec(memory_space=pltpu.VMEM), pl.BlockSpec(memory_space=pltpu.VMEM)),
        scratch_shapes=[
            vm((depth + 8, own, nx), F32),
            vm((depth + 8, own, nx), F32),
            vm((2, 2, depth, own, nx), F32),
            vm((depth, own, nx), F32),
            vm((2, depth, own, nx), F32),
            vm((depth, 16, nx), F32),
            vm((depth, 8, nx), F32),
            vm((3, GROUP, depth, own, nx), F32),
            vm((depth + 8, rows + 16, nx), F32),
            vm((depth + 8, rows + 16, nx), F32),
            vm((depth, rows, nx), F32),
            vm((depth, rows, nx), F32),
            vm((depth, rows, nx), F32),
            vm((2, 2, depth, own, nx), F32),
            vm((2, 2, depth, own, nx), F32),
            vm((2, depth // 2, own, nx), F32),
            vm((depth, 2, 8, nx), F32),
            vm((nx, nx), jnp.bfloat16),
            dma((3, 8)), dma((3, 8)), dma((2, 6)), dma((2, 4, 2)), dma((2, 4, 3)), dma((2, 4, 2)), dma((7,)),
        ],
        compiler_params=pltpu.CompilerParams(
            collective_id=0, has_side_effects=True, vmem_limit_bytes=48 * 1024 * 1024
        ),
        name="born",
    )(*(pltpu.with_memory_space_constraint(v, pltpu.HBM) for v in (iprev, inow, forcing, stiff, pprev, pnow, pert))))


def hand_over(a, b, a_out, b_out, sems):
    moves = [pltpu.make_async_copy(a, a_out, sems.at[0]), pltpu.make_async_copy(b, b_out, sems.at[1])]
    for m in moves:
        m.start()
    for m in moves:
        m.wait()


def fresh(a, b):
    vmem, any_ = pl.BlockSpec(memory_space=pltpu.VMEM), pl.BlockSpec(memory_space=pl.ANY)
    return pl.pallas_call(
        hand_over,
        out_shape=(jax.ShapeDtypeStruct(a.shape, F32), jax.ShapeDtypeStruct(b.shape, F32)),
        in_specs=[vmem, vmem], out_specs=(any_, any_), name="fresh",
        scratch_shapes=[pltpu.SemaphoreType.DMA((2,))],
    )(pltpu.with_memory_space_constraint(a, pltpu.VMEM), pltpu.with_memory_space_constraint(b, pltpu.VMEM))


def solution(mesh):
    spec = P("slab", "probe", None)
    return jax.shard_map(
        functools.partial(local, mesh.shape["probe"], mesh.shape["slab"]),
        mesh=mesh,
        in_specs=(spec, spec, P(None, "slab", "probe", None), spec, spec, spec, spec),
        out_specs=(spec, spec),
        check_vma=False,
    )
```

```python
import functools

import jax
import jax.numpy as jnp
from jax import lax
from jax.experimental import pallas as pl
from jax.experimental.pallas import tpu as pltpu
from jax.sharding import PartitionSpec as P

coefficients = (-205.0 / 72.0, 8.0 / 5.0, -1.0 / 5.0, 8.0 / 315.0, -1.0 / 560.0)
SCALE = 5040
BAND = (0.0, 8064.0, -1008.0, 128.0, -9.0)

GROUP = 8
REACH = 4
MESH = pl.DeviceIdType.MESH
RELAYED = (True, False)
ORDER = (
    "rims_u0", "own_s_away", "depth_0", "pack", "constants", "pass_u0", "own_s_along", "incident_0", "rims_u1", "own_0", "fwd_s0", "fwd_s1", "fwd_s2", "hear_0", "lap_00", "lap_01", "fwd_00_inner", "fwd_01_inner", "rims_0", "pass_0", "incident_1", "own_1", "fwd_00_outer", "fwd_01_outer", "fwd_02", "loads", "new_00", "new_07", "new_01", "new_02", "new_03", "new_04", "new_05", "new_06", "depth_1", "fwd_10", "fwd_11", "rims_1", "hear_1", "lap_10", "lap_11", "fwd_12", "pass_1", "new_11", "new_12", "new_13", "new_14", "new_15", "new_16", "new_10", "new_17",
)
F32 = jnp.float32


def kernel(
    depth, rows, nx, n_probe, n_slab,
    iprev, inow, forcing, stiff, pprev, pnow, pert,
    probe_out, inc_out,
    U0, U1, UH, IP, FO, YE, XS, G, E0, E1, PP, PT, L, SB, DH, RX, CL, B,
    ssG, rsG, ssU, rsU, ssD, rsD, ls,
):
    Pi = lax.axis_index("probe")
    Si = lax.axis_index("slab")
    p = Pi % GROUP
    zl = p // 2
    yl = p % 2
    z1 = zl + 1 - 2 * (zl % 2)
    z2 = (zl + 2) % 4
    z3 = 3 - zl
    base = Pi - p
    inner = jnp.logical_or(zl == 1, zl == 2)
    partner = Pi + 1 - 2 * yl
    own = rows // GROUP

    def zdev(k):
        return (base + (z1, z2, z3)[k] * 2 + yl, Si)

    def zslot(k):
        return (z1, z2, z3)[k] * 2 + yl

    has_p_lo, has_p_hi = Pi > 0, Pi < n_probe - 1
    has_b_lo, has_b_hi = Pi >= GROUP, Pi < n_probe - GROUP
    has_s_lo, has_s_hi = Si > 0, Si < n_slab - 1
    block, last = Pi // GROUP, n_probe // GROUP - 1
    from_lo, relay_lo, to_lo = block == 2, block == 0, block == 1
    from_hi, relay_hi, to_hi = block == last - 2, block == last, block == last - 1

    loads = [
        pltpu.make_async_copy(inow, U0.at[pl.ds(REACH, depth)], ls.at[0]),
        pltpu.make_async_copy(stiff, G.at[0, p], ls.at[1]),
        pltpu.make_async_copy(pnow, E0.at[pl.ds(REACH, depth), pl.ds(8, rows)], ls.at[2]),
        pltpu.make_async_copy(iprev, IP, ls.at[3]),
        pltpu.make_async_copy(forcing, FO, ls.at[4]),
        pltpu.make_async_copy(pprev, PP, ls.at[5]),
        pltpu.make_async_copy(pert, PT, ls.at[6]),
    ]
    for c in loads:
        c.start()

    bar = pltpu.get_barrier_semaphore()

    def hello(dev):
        pl.semaphore_signal(bar, inc=1, device_id=dev, device_id_type=MESH)

    for k in range(3):
        hello(zdev(k))
    hello((partner, Si))
    sides = [
        (has_p_lo, (Pi - 1, Si)), (has_p_hi, (Pi + 1, Si)),
        (has_b_lo, (Pi - GROUP, Si)), (has_b_hi, (Pi + GROUP, Si)),
        (has_s_lo, (Pi, Si - 1)), (has_s_hi, (Pi, Si + 1)),
        (Pi > 1, (Pi - 2, Si)), (Pi < n_probe - 2, (Pi + 2, Si)),
        (jnp.logical_or(from_lo, relay_hi), (Pi - 2 * GROUP, Si)),
        (jnp.logical_or(from_hi, relay_lo), (Pi + 2 * GROUP, Si)),
    ]
    for cond, dev in sides:
        pl.when(cond)(functools.partial(hello, dev))
    peers = 4
    for cond, _ in sides:
        peers = peers + cond.astype(jnp.int32)
    pl.semaphore_wait(bar, peers)

    def remote(src, dst, ssem, rsem, dev):
        return pltpu.make_async_remote_copy(
            src_ref=src, dst_ref=dst, send_sem=ssem, recv_sem=rsem,
            device_id=dev, device_id_type=MESH,
        )

    pending = []

    def send(cond, desc):
        if cond is None:
            desc.start()
        else:
            pl.when(cond)(desc.start)
        pending.append((cond, desc))

    half = depth // 2
    near, far = pl.ds(0, half), pl.ds(half, half)
    lower, upper = yl == 0, yl == 1

    def rims_incident(step, src, U):
        def to(cond, dev, side, part, k):
            send(cond, remote(src.at[part], UH.at[step, side, part], ssU.at[step, k], rsU.at[step, side, k % 2], dev))

        for part, k in ((near, 0), (far, 1)):
            to(lower, (partner, Si), 0, part, k)
            to(upper, (partner, Si), 1, part, k)
        send(has_s_lo, remote(src.at[pl.ds(0, REACH)], U.at[pl.ds(depth + REACH, REACH)],
                              ssU.at[step, 4], rsU.at[step, 3, 0], (Pi, Si - 1)))
        send(has_s_hi, remote(src.at[pl.ds(depth - REACH, REACH)], U.at[pl.ds(0, REACH)],
                              ssU.at[step, 5], rsU.at[step, 2, 0], (Pi, Si + 1)))
        for part, k in () if RELAYED[step] else ((near, 2), (far, 3)):
            to(jnp.logical_and(lower, has_p_lo), (Pi - 1, Si), 1, part, k)
            to(jnp.logical_and(upper, has_p_hi), (Pi + 1, Si), 0, part, k)

    def arrived(step, side, k):
        r = UH.at[step, side, (near, far)[k]]
        remote(r, r, ssU.at[step, 3], rsU.at[step, side, k], (partner, Si)).wait_recv()

    def pass_incident(step):
        for mine, there, side, dev in (
            (lower, Pi < n_probe - 2, 1, (Pi + 2, Si)),
            (upper, Pi > 1, 0, (Pi - 2, Si)),
        ):
            for part, k in ((near, 0), (far, 1)):
                pl.when(mine)(functools.partial(arrived, step, side, k))
                send(jnp.logical_and(mine, there),
                     remote(UH.at[step, side, part], UH.at[step, 1 - side, part], ssU.at[step, 2 + k],
                            rsU.at[step, 1 - side, k], dev))

    def wait_incident(step, U):
        for mine, side, there in ((lower, 1, has_p_lo), (upper, 0, has_p_hi)):

            @pl.when(mine)
            def _(side=side):
                if not RELAYED[step]:
                    arrived(step, side, 0)
                    arrived(step, side, 1)

            @pl.when(jnp.logical_and(mine, there))
            def _(side=side):
                arrived(step, 1 - side, 0)
                arrived(step, 1 - side, 1)

        for side, cond, at in ((2, has_s_lo, 0), (3, has_s_hi, depth + REACH)):
            r = U.at[pl.ds(at, REACH)]
            d = remote(r, r, ssU.at[step, 3], rsU.at[step, side, 0], (partner, Si))
            pl.when(cond)(d.wait_recv)

    def send_depth(step, low, high, E):
        send(has_s_lo, remote(low, E.at[pl.ds(depth + REACH, REACH), pl.ds(8, rows)],
                              ssD.at[step, 2, 0], rsD.at[step, 3, 0], (Pi, Si - 1)))
        send(has_s_hi, remote(high, E.at[pl.ds(0, REACH), pl.ds(8, rows)],
                              ssD.at[step, 3, 0], rsD.at[step, 2, 0], (Pi, Si + 1)))

    def wait_depth(step, E):
        for side, cond, at in ((2, has_s_lo, 0), (3, has_s_hi, depth + REACH)):
            r = E.at[pl.ds(at, REACH), pl.ds(8, rows)]
            d = remote(r, r, ssD.at[step, side, 0], rsD.at[step, side, 0], (partner, Si))
            pl.when(cond)(d.wait_recv)

    def send_rim(step, side, role=None):
        cond, by_x, shift, hop = (
            (has_b_lo, from_lo, -GROUP, -2 * GROUP), (has_b_hi, from_hi, GROUP, 2 * GROUP)
        )[side]
        if role is not None:
            cond, by_x = jnp.logical_and(cond, role), jnp.logical_and(by_x, role)

        def to(cond, dst, part, k, rsem, dev):
            send(cond, remote(SB.at[step, side, part], dst, ssD.at[step, side, k], rsem, dev))

        out = DH.at[step, 1 - side]
        to(cond, out.at[near], near, 0, rsD.at[step, 1 - side, 0], (Pi + shift, Si))
        to(jnp.logical_and(cond, jnp.logical_not(by_x)), out.at[far], far, 1,
           rsD.at[step, 1 - side, 1], (Pi + shift, Si))
        to(by_x, RX.at[step], far, 2, rsD.at[step, 2, 1], (Pi + hop, Si))

    def pass_rim(step):
        for cond, side, shift in ((relay_lo, 1, GROUP), (relay_hi, 0, -GROUP)):

            @pl.when(cond)
            def _():
                remote(RX.at[step], RX.at[step], ssD.at[step, 3, 1], rsD.at[step, 2, 1], (partner, Si)).wait_recv()

            send(cond, remote(RX.at[step], DH.at[step, side, far], ssD.at[step, 2, 1], rsD.at[step, side, 1],
                              (Pi + shift, Si)))

    def wait_rim(step, side):
        for part, k in ((near, 0), (far, 1)):
            r = DH.at[step, side, part]
            d = remote(r, r, ssD.at[step, side, k], rsD.at[step, side, k], (partner, Si))
            pl.when((has_b_lo, has_b_hi)[side])(d.wait_recv)

    def gather_own(a, src, part="all"):
        dst = G.at[a, p]
        for k, up, there in ((0, zl % 2 == 0, None), (1, zl < 2, None), (2, zl == 1, inner)):
            if part != "all":
                way = (up == upper) if part == "away" else (up != upper)
                there = way if there is None else jnp.logical_and(there, way)
            send(there, remote(src, dst, ssG.at[a, 1 + k], rsG.at[a, p], zdev(k)))
        if part != "along":
            send(None, remote(src, dst, ssG.at[a, 0], rsG.at[a, p], (partner, Si)))

    def forward(a, k, role=None):
        slot = zslot(k)
        r = G.at[a, slot]
        arrival = remote(r, r, ssG.at[a, 4 + k], rsG.at[a, slot], (partner, Si))
        if role is None:
            arrival.wait_recv()
        else:
            pl.when(role)(arrival.wait_recv)
        if k == 1:
            relay = inner if role is None else jnp.logical_and(inner, role)
            send(relay, remote(r, r, ssG.at[a, 7], rsG.at[a, slot], zdev(0)))
        send(role, remote(r, r, ssG.at[a, 4 + k], rsG.at[a, slot], (partner, Si)))

    def gather_wait(a, q):
        r = G.at[a, q]
        d = remote(r, r, ssG.at[a, 0], rsG.at[a, q], (partner, Si))
        pl.when((q % 2) != yl)(d.wait_recv)

    def pack():
        loads[2].wait()

        def row(z, _):
            SB[0, 0, z] = E0[z + REACH, 8:12, :]
            SB[0, 1, z] = E0[z + REACH, rows + 4:rows + 8, :]
            return 0

        lax.fori_loop(0, depth, row, 0)

    def constants():
        def band(i, _):
            r = lax.broadcasted_iota(jnp.int32, (64, nx), 0) + i * 64
            c = lax.broadcasted_iota(jnp.int32, (64, nx), 1)
            gap = jnp.abs(r - c)
            v = jnp.zeros((64, nx), F32)
            for j in range(1, 5):
                v = jnp.where(gap == j, BAND[j], v)
            B[pl.ds(pl.multiple_of(i * 64, 64), 64), :] = v.astype(jnp.bfloat16)
            return 0

        lax.fori_loop(0, nx // 64, band, 0)

        edge = jnp.zeros((8, nx), F32)

        def clear(z, _):
            for E in (E0, E1):
                E[z + REACH, 0:8, :] = edge
                E[z + REACH, rows + 8:rows + 16, :] = edge
            CL[z, 0, :, :] = edge
            CL[z, 1, :, :] = edge
            return 0

        lax.fori_loop(0, depth, clear, 0)
        for cond, at in ((has_s_lo, 0), (has_s_hi, depth + REACH)):

            @pl.when(jnp.logical_not(cond))
            def _(at=at):
                for i in range(REACH):
                    for E in (E0, E1):
                        E[at + i, 8:8 + rows, :] = jnp.zeros((rows, nx), F32)
                    for U in (U0, U1):
                        U[at + i] = jnp.zeros((own, nx), F32)

        for side, cp, cb in ((0, has_p_lo, has_b_lo), (1, has_p_hi, has_b_hi)):
            for R, cond in ((UH, cp), (DH, cb)):

                @pl.when(jnp.logical_not(cond))
                def _(R=R, side=side):
                    def zero(z, _):
                        for step in range(2):
                            R[step, side, z] = jnp.zeros((own, nx), F32)
                        return 0

                    lax.fori_loop(0, depth, zero, 0)

    def along_x(D):
        hi = D.astype(jnp.bfloat16)
        lo = (D - hi.astype(F32)).astype(jnp.bfloat16)
        X = jnp.dot(hi, B[...], preferred_element_type=F32)
        X = X + jnp.dot(lo, B[...], preferred_element_type=F32)
        return X * (1.0 / SCALE)

    def incident(step, U, older, into):
        def build(z, _):
            YE[z, 4:8, :] = UH[step, 0, z]
            YE[z, 8:12, :] = U[z + REACH]
            YE[z, 12:16, :] = UH[step, 1, z]
            return 0

        lax.fori_loop(0, depth, build, 0)
        XS[...] = along_x(YE[:, 8:16, :].reshape(depth * 8, nx)).reshape(depth, 8, nx)

        def point(z, _):
            c = U[z + REACH]
            acc = XS[z, 0:4, :] + (3.0 * coefficients[0]) * c
            for j in range(1, 5):
                acc = acc + coefficients[j] * (U[z + REACH - j] + U[z + REACH + j])
            for j in range(1, 5):
                acc = acc + coefficients[j] * (YE[z, 8 - j:12 - j, :] + YE[z, 8 + j:12 + j, :])
            G[1 + step, p, z] = acc
            into(z, 2.0 * c - older(z) + G[0, p, z] * acc + FO[step, z])
            return 0

        lax.fori_loop(0, depth, point, 0)

    def laplace(E, part, parts):
        first, end = part * depth // parts, (part + 1) * depth // parts

        def wide(c, _):
            z0 = c * 8
            D = E[pl.ds(z0 + REACH, 8), 8:8 + rows, :].reshape(8 * rows, nx)
            L[pl.ds(z0, 8)] = along_x(D).reshape(8, rows, nx)
            return 0

        lax.fori_loop(first // 8, end // 8, wide, 0)

        def point(z, _):
            acc = L[z] + (3.0 * coefficients[0]) * E[z + REACH, 8:8 + rows, :]
            for j in range(1, 5):
                acc = acc + coefficients[j] * (E[z + REACH - j, 8:8 + rows, :] + E[z + REACH + j, 8:8 + rows, :])
            for j in range(1, 5):
                acc = acc + coefficients[j] * (
                    E[z + REACH, 8 - j:8 - j + rows, :] + E[z + REACH, 8 + j:8 + j + rows, :]
                )
            L[z] = acc
            return 0

        lax.fori_loop(first, end, point, 0)

    def update(step, q, newer, older, into):
        gather_wait(0, q) if step == 0 else None
        gather_wait(1 + step, q)
        side = 0 if q == 0 else 1 if q == GROUP - 1 else None
        if side is not None:
            wait_rim(step, side)
        at = q * own

        def point(z, _):
            lap = L[z, at:at + own, :]
            if side == 0:
                CL[z, 0, 0:4, :] = DH[step, 0, z]
                for j in range(1, 5):
                    lap = lap + coefficients[j] * CL[z, 0, 4 - j:8 - j, :]
            if side == 1:
                CL[z, 1, 4:8, :] = DH[step, 1, z]
                for j in range(1, 5):
                    lap = lap + coefficients[j] * CL[z, 1, j:j + 4, :]
            value = (
                2.0 * newer(z, at) - older(z, at)
                + G[0, q, z] * (lap + 2.0 * PT[z, at:at + own, :] * G[1 + step, q, z])
            )
            into(z, at, value)
            if step == 0 and side is not None:
                SB[1, side, z] = value
            return 0

        lax.fori_loop(0, depth, point, 0, unroll=4)

    def into_u1(z, v):
        U1[z + REACH] = v

    def into_out(z, v):
        inc_out[z] = v

    def into_e1(z, at, v):
        E1[z + REACH, 8 + at:8 + at + own, :] = v

    def into_probe(z, at, v):
        probe_out[z, at:at + own, :] = v

    def from_e(E):
        return lambda z, at: E[z + REACH, 8 + at:8 + at + own, :]

    def incident_0():
        for i in (0, 1, 3, 4):
            loads[i].wait()
        wait_incident(0, U0)
        incident(0, U0, lambda z: IP[z], into_u1)

    def incident_1():
        wait_incident(1, U1)
        incident(1, U1, lambda z: U0[z + REACH], into_out)

    def update_0(q):
        update(0, q, from_e(E0), lambda z, at: PP[z, at:at + own, :], into_e1)

    def update_1(q):
        update(1, q, from_e(E1), from_e(E0), into_probe)

    low, high = pl.ds(REACH, REACH), pl.ds(depth, REACH)
    tasks = {
        "rims_u0": lambda: rims_incident(0, inow, U0),
        "rims_u1": lambda: rims_incident(1, U1.at[pl.ds(REACH, depth)], U1),
        "pass_u0": lambda: pass_incident(0),
        "pass_u1": lambda: pass_incident(1),
        "own_s": lambda: gather_own(0, stiff),
        "own_s_away": lambda: gather_own(0, stiff, "away"),
        "own_s_along": lambda: gather_own(0, stiff, "along"),
        "own_0_away": lambda: gather_own(1, G.at[1, p], "away"),
        "own_0_along": lambda: gather_own(1, G.at[1, p], "along"),
        "own_0": lambda: gather_own(1, G.at[1, p]),
        "own_1": lambda: gather_own(2, G.at[2, p]),
        "depth_0": lambda: send_depth(0, pnow.at[pl.ds(0, REACH)], pnow.at[pl.ds(depth - REACH, REACH)], E0),
        "depth_1": lambda: send_depth(1, E1.at[low, pl.ds(8, rows)], E1.at[high, pl.ds(8, rows)], E1),
        "pack": pack,
        "constants": constants,
        "rims_0": lambda: (send_rim(0, 0), send_rim(0, 1)),
        "rims_1": lambda: (send_rim(1, 0), send_rim(1, 1)),
        "pass_0": lambda: pass_rim(0),
        "pass_1": lambda: pass_rim(1),
        "incident_0": incident_0,
        "incident_1": incident_1,
        "hear_0": lambda: wait_depth(0, E0),
        "hear_1": lambda: wait_depth(1, E1),
        "loads": lambda: (loads[5].wait(), loads[6].wait()),
    }
    outer = jnp.logical_not(inner)
    for k in range(3):
        for a, name in enumerate("s01"):
            tasks["fwd_%s%d" % (name, k)] = functools.partial(forward, a, k)
            tasks["fwd_%s%d_inner" % (name, k)] = functools.partial(forward, a, k, inner)
            tasks["fwd_%s%d_outer" % (name, k)] = functools.partial(forward, a, k, outer)
    for step in range(2):
        tasks["rims_%d_inner" % step] = lambda step=step: (send_rim(step, 0, inner), send_rim(step, 1, inner))
        tasks["rims_%d_outer" % step] = lambda step=step: (send_rim(step, 0, outer), send_rim(step, 1, outer))
    for part in range(2):
        tasks["lap_0%d" % part] = functools.partial(laplace, E0, part, 2)
        tasks["lap_1%d" % part] = functools.partial(laplace, E1, part, 2)
    for q in range(GROUP):
        tasks["new_0%d" % q] = functools.partial(update_0, q)
        tasks["new_1%d" % q] = functools.partial(update_1, q)
    for name in ORDER:
        tasks[name]()

    for cond, d in pending:
        if cond is None:
            d.wait_send()
        else:
            pl.when(cond)(d.wait_send)


def local(n_probe, n_slab, iprev, inow, forcing, stiff, pprev, pnow, pert):
    depth, own, nx = inow.shape
    rows = pnow.shape[1]
    dma = pltpu.SemaphoreType.DMA
    vm = pltpu.VMEM
    return fresh(*pl.pallas_call(
        functools.partial(kernel, depth, rows, nx, n_probe, n_slab),
        out_shape=(pltpu.VMEM(pnow.shape, F32), pltpu.VMEM(inow.shape, F32)),
        in_specs=[pl.BlockSpec(memory_space=pltpu.HBM)] * 7,
        out_specs=(pl.BlockSpec(memory_space=pltpu.VMEM), pl.BlockSpec(memory_space=pltpu.VMEM)),
        scratch_shapes=[
            vm((depth + 8, own, nx), F32),
            vm((depth + 8, own, nx), F32),
            vm((2, 2, depth, own, nx), F32),
            vm((depth, own, nx), F32),
            vm((2, depth, own, nx), F32),
            vm((depth, 16, nx), F32),
            vm((depth, 8, nx), F32),
            vm((3, GROUP, depth, own, nx), F32),
            vm((depth + 8, rows + 16, nx), F32),
            vm((depth + 8, rows + 16, nx), F32),
            vm((depth, rows, nx), F32),
            vm((depth, rows, nx), F32),
            vm((depth, rows, nx), F32),
            vm((2, 2, depth, own, nx), F32),
            vm((2, 2, depth, own, nx), F32),
            vm((2, depth // 2, own, nx), F32),
            vm((depth, 2, 8, nx), F32),
            vm((nx, nx), jnp.bfloat16),
            dma((3, 8)), dma((3, 8)), dma((2, 6)), dma((2, 4, 2)), dma((2, 4, 3)), dma((2, 4, 2)), dma((7,)),
        ],
        compiler_params=pltpu.CompilerParams(
            collective_id=0, has_side_effects=True, vmem_limit_bytes=48 * 1024 * 1024
        ),
        name="born",
    )(*(pltpu.with_memory_space_constraint(v, pltpu.HBM) for v in (iprev, inow, forcing, stiff, pprev, pnow, pert))))


def hand_over(a, b, a_out, b_out, sems):
    moves = [pltpu.make_async_copy(a, a_out, sems.at[0]), pltpu.make_async_copy(b, b_out, sems.at[1])]
    for m in moves:
        m.start()
    for m in moves:
        m.wait()


def fresh(a, b):
    vmem, any_ = pl.BlockSpec(memory_space=pltpu.VMEM), pl.BlockSpec(memory_space=pl.ANY)
    return pl.pallas_call(
        hand_over,
        out_shape=(jax.ShapeDtypeStruct(a.shape, F32), jax.ShapeDtypeStruct(b.shape, F32)),
        in_specs=[vmem, vmem], out_specs=(any_, any_), name="fresh",
        scratch_shapes=[pltpu.SemaphoreType.DMA((2,))],
    )(pltpu.with_memory_space_constraint(a, pltpu.VMEM), pltpu.with_memory_space_constraint(b, pltpu.VMEM))


def solution(mesh):
    spec = P("slab", "probe", None)
    return jax.shard_map(
        functools.partial(local, mesh.shape["probe"], mesh.shape["slab"]),
        mesh=mesh,
        in_specs=(spec, spec, P(None, "slab", "probe", None), spec, spec, spec, spec),
        out_specs=(spec, spec),
        check_vma=False,
    )
```

```python
import functools

import jax
import jax.numpy as jnp
from jax import lax
from jax.experimental import pallas as pl
from jax.experimental.pallas import tpu as pltpu
from jax.sharding import PartitionSpec as P

coefficients = (-205.0 / 72.0, 8.0 / 5.0, -1.0 / 5.0, 8.0 / 315.0, -1.0 / 560.0)
SCALE = 5040
BAND = (0.0, 8064.0, -1008.0, 128.0, -9.0)

GROUP = 8
REACH = 4
MESH = pl.DeviceIdType.MESH
RELAYED = (True, False)
ORDER = (
    "rims_u0", "own_s_away", "depth_0", "pack", "constants", "pass_u0", "own_s_along", "incident_0", "rims_u1", "own_0", "fwd_s0", "fwd_s1", "fwd_s2", "hear_0", "fwd_00_inner", "fwd_01_inner", "rims_0", "lap_00", "lap_01", "pass_0", "incident_1", "own_1", "fwd_00_outer", "fwd_01_outer", "fwd_02", "loads", "new_00", "new_07", "new_01", "new_02", "new_03", "new_04", "new_05", "new_06", "depth_1", "fwd_10", "fwd_11", "rims_1", "hear_1", "lap_10", "lap_11", "fwd_12", "pass_1", "new_11", "new_12", "new_13", "new_14", "new_15", "new_16", "new_10", "new_17",
)
F32 = jnp.float32


def kernel(
    depth, rows, nx, n_probe, n_slab,
    iprev, inow, forcing, stiff, pprev, pnow, pert,
    probe_out, inc_out,
    U0, U1, UH, IP, FO, YE, XS, G, E0, E1, PP, PT, L, SB, DH, RX, CL, B,
    ssG, rsG, ssU, rsU, ssD, rsD, ls,
):
    Pi = lax.axis_index("probe")
    Si = lax.axis_index("slab")
    p = Pi % GROUP
    zl = p // 2
    yl = p % 2
    z1 = zl + 1 - 2 * (zl % 2)
    z2 = (zl + 2) % 4
    z3 = 3 - zl
    base = Pi - p
    inner = jnp.logical_or(zl == 1, zl == 2)
    partner = Pi + 1 - 2 * yl
    own = rows // GROUP

    def zdev(k):
        return (base + (z1, z2, z3)[k] * 2 + yl, Si)

    def zslot(k):
        return (z1, z2, z3)[k] * 2 + yl

    has_p_lo, has_p_hi = Pi > 0, Pi < n_probe - 1
    has_b_lo, has_b_hi = Pi >= GROUP, Pi < n_probe - GROUP
    has_s_lo, has_s_hi = Si > 0, Si < n_slab - 1
    block, last = Pi // GROUP, n_probe // GROUP - 1
    from_lo, relay_lo, to_lo = block == 2, block == 0, block == 1
    from_hi, relay_hi, to_hi = block == last - 2, block == last, block == last - 1

    loads = [
        pltpu.make_async_copy(inow, U0.at[pl.ds(REACH, depth)], ls.at[0]),
        pltpu.make_async_copy(stiff, G.at[0, p], ls.at[1]),
        pltpu.make_async_copy(pnow, E0.at[pl.ds(REACH, depth), pl.ds(8, rows)], ls.at[2]),
        pltpu.make_async_copy(iprev, IP, ls.at[3]),
        pltpu.make_async_copy(forcing, FO, ls.at[4]),
        pltpu.make_async_copy(pprev, PP, ls.at[5]),
        pltpu.make_async_copy(pert, PT, ls.at[6]),
    ]
    for c in loads:
        c.start()

    bar = pltpu.get_barrier_semaphore()

    def hello(dev):
        pl.semaphore_signal(bar, inc=1, device_id=dev, device_id_type=MESH)

    for k in range(3):
        hello(zdev(k))
    hello((partner, Si))
    sides = [
        (has_p_lo, (Pi - 1, Si)), (has_p_hi, (Pi + 1, Si)),
        (has_b_lo, (Pi - GROUP, Si)), (has_b_hi, (Pi + GROUP, Si)),
        (has_s_lo, (Pi, Si - 1)), (has_s_hi, (Pi, Si + 1)),
        (Pi > 1, (Pi - 2, Si)), (Pi < n_probe - 2, (Pi + 2, Si)),
        (jnp.logical_or(from_lo, relay_hi), (Pi - 2 * GROUP, Si)),
        (jnp.logical_or(from_hi, relay_lo), (Pi + 2 * GROUP, Si)),
    ]
    for cond, dev in sides:
        pl.when(cond)(functools.partial(hello, dev))
    peers = 4
    for cond, _ in sides:
        peers = peers + cond.astype(jnp.int32)
    pl.semaphore_wait(bar, peers)

    def remote(src, dst, ssem, rsem, dev):
        return pltpu.make_async_remote_copy(
            src_ref=src, dst_ref=dst, send_sem=ssem, recv_sem=rsem,
            device_id=dev, device_id_type=MESH,
        )

    pending = []

    def send(cond, desc):
        if cond is None:
            desc.start()
        else:
            pl.when(cond)(desc.start)
        pending.append((cond, desc))

    half = depth // 2
    near, far = pl.ds(0, half), pl.ds(half, half)
    lower, upper = yl == 0, yl == 1

    def rims_incident(step, src, U):
        def to(cond, dev, side, part, k):
            send(cond, remote(src.at[part], UH.at[step, side, part], ssU.at[step, k], rsU.at[step, side, k % 2], dev))

        for part, k in ((near, 0), (far, 1)):
            to(lower, (partner, Si), 0, part, k)
            to(upper, (partner, Si), 1, part, k)
        send(has_s_lo, remote(src.at[pl.ds(0, REACH)], U.at[pl.ds(depth + REACH, REACH)],
                              ssU.at[step, 4], rsU.at[step, 3, 0], (Pi, Si - 1)))
        send(has_s_hi, remote(src.at[pl.ds(depth - REACH, REACH)], U.at[pl.ds(0, REACH)],
                              ssU.at[step, 5], rsU.at[step, 2, 0], (Pi, Si + 1)))
        for part, k in () if RELAYED[step] else ((near, 2), (far, 3)):
            to(jnp.logical_and(lower, has_p_lo), (Pi - 1, Si), 1, part, k)
            to(jnp.logical_and(upper, has_p_hi), (Pi + 1, Si), 0, part, k)

    def arrived(step, side, k):
        r = UH.at[step, side, (near, far)[k]]
        remote(r, r, ssU.at[step, 3], rsU.at[step, side, k], (partner, Si)).wait_recv()

    def pass_incident(step):
        for mine, there, side, dev in (
            (lower, Pi < n_probe - 2, 1, (Pi + 2, Si)),
            (upper, Pi > 1, 0, (Pi - 2, Si)),
        ):
            for part, k in ((near, 0), (far, 1)):
                pl.when(mine)(functools.partial(arrived, step, side, k))
                send(jnp.logical_and(mine, there),
                     remote(UH.at[step, side, part], UH.at[step, 1 - side, part], ssU.at[step, 2 + k],
                            rsU.at[step, 1 - side, k], dev))

    def wait_incident(step, U):
        for mine, side, there in ((lower, 1, has_p_lo), (upper, 0, has_p_hi)):

            @pl.when(mine)
            def _(side=side):
                if not RELAYED[step]:
                    arrived(step, side, 0)
                    arrived(step, side, 1)

            @pl.when(jnp.logical_and(mine, there))
            def _(side=side):
                arrived(step, 1 - side, 0)
                arrived(step, 1 - side, 1)

        for side, cond, at in ((2, has_s_lo, 0), (3, has_s_hi, depth + REACH)):
            r = U.at[pl.ds(at, REACH)]
            d = remote(r, r, ssU.at[step, 3], rsU.at[step, side, 0], (partner, Si))
            pl.when(cond)(d.wait_recv)

    def send_depth(step, low, high, E):
        send(has_s_lo, remote(low, E.at[pl.ds(depth + REACH, REACH), pl.ds(8, rows)],
                              ssD.at[step, 2, 0], rsD.at[step, 3, 0], (Pi, Si - 1)))
        send(has_s_hi, remote(high, E.at[pl.ds(0, REACH), pl.ds(8, rows)],
                              ssD.at[step, 3, 0], rsD.at[step, 2, 0], (Pi, Si + 1)))

    def wait_depth(step, E):
        for side, cond, at in ((2, has_s_lo, 0), (3, has_s_hi, depth + REACH)):
            r = E.at[pl.ds(at, REACH), pl.ds(8, rows)]
            d = remote(r, r, ssD.at[step, side, 0], rsD.at[step, side, 0], (partner, Si))
            pl.when(cond)(d.wait_recv)

    def send_rim(step, side, role=None):
        cond, by_x, shift, hop = (
            (has_b_lo, from_lo, -GROUP, -2 * GROUP), (has_b_hi, from_hi, GROUP, 2 * GROUP)
        )[side]
        if role is not None:
            cond, by_x = jnp.logical_and(cond, role), jnp.logical_and(by_x, role)

        def to(cond, dst, part, k, rsem, dev):
            send(cond, remote(SB.at[step, side, part], dst, ssD.at[step, side, k], rsem, dev))

        out = DH.at[step, 1 - side]
        to(cond, out.at[near], near, 0, rsD.at[step, 1 - side, 0], (Pi + shift, Si))
        to(jnp.logical_and(cond, jnp.logical_not(by_x)), out.at[far], far, 1,
           rsD.at[step, 1 - side, 1], (Pi + shift, Si))
        to(by_x, RX.at[step], far, 2, rsD.at[step, 2, 1], (Pi + hop, Si))

    def pass_rim(step):
        for cond, side, shift in ((relay_lo, 1, GROUP), (relay_hi, 0, -GROUP)):

            @pl.when(cond)
            def _():
                remote(RX.at[step], RX.at[step], ssD.at[step, 3, 1], rsD.at[step, 2, 1], (partner, Si)).wait_recv()

            send(cond, remote(RX.at[step], DH.at[step, side, far], ssD.at[step, 2, 1], rsD.at[step, side, 1],
                              (Pi + shift, Si)))

    def wait_rim(step, side):
        for part, k in ((near, 0), (far, 1)):
            r = DH.at[step, side, part]
            d = remote(r, r, ssD.at[step, side, k], rsD.at[step, side, k], (partner, Si))
            pl.when((has_b_lo, has_b_hi)[side])(d.wait_recv)

    def gather_own(a, src, part="all"):
        dst = G.at[a, p]
        for k, up, there in ((0, zl % 2 == 0, None), (1, zl < 2, None), (2, zl == 1, inner)):
            if part != "all":
                way = (up == upper) if part == "away" else (up != upper)
                there = way if there is None else jnp.logical_and(there, way)
            send(there, remote(src, dst, ssG.at[a, 1 + k], rsG.at[a, p], zdev(k)))
        if part != "along":
            send(None, remote(src, dst, ssG.at[a, 0], rsG.at[a, p], (partner, Si)))

    def forward(a, k, role=None):
        slot = zslot(k)
        r = G.at[a, slot]
        arrival = remote(r, r, ssG.at[a, 4 + k], rsG.at[a, slot], (partner, Si))
        if role is None:
            arrival.wait_recv()
        else:
            pl.when(role)(arrival.wait_recv)
        if k == 1:
            relay = inner if role is None else jnp.logical_and(inner, role)
            send(relay, remote(r, r, ssG.at[a, 7], rsG.at[a, slot], zdev(0)))
        send(role, remote(r, r, ssG.at[a, 4 + k], rsG.at[a, slot], (partner, Si)))

    def gather_wait(a, q):
        r = G.at[a, q]
        d = remote(r, r, ssG.at[a, 0], rsG.at[a, q], (partner, Si))
        pl.when((q % 2) != yl)(d.wait_recv)

    def pack():
        loads[2].wait()

        def row(z, _):
            SB[0, 0, z] = E0[z + REACH, 8:12, :]
            SB[0, 1, z] = E0[z + REACH, rows + 4:rows + 8, :]
            return 0

        lax.fori_loop(0, depth, row, 0)

    def constants():
        def band(i, _):
            r = lax.broadcasted_iota(jnp.int32, (64, nx), 0) + i * 64
            c = lax.broadcasted_iota(jnp.int32, (64, nx), 1)
            gap = jnp.abs(r - c)
            v = jnp.zeros((64, nx), F32)
            for j in range(1, 5):
                v = jnp.where(gap == j, BAND[j], v)
            B[pl.ds(pl.multiple_of(i * 64, 64), 64), :] = v.astype(jnp.bfloat16)
            return 0

        lax.fori_loop(0, nx // 64, band, 0)

        edge = jnp.zeros((8, nx), F32)

        def clear(z, _):
            for E in (E0, E1):
                E[z + REACH, 0:8, :] = edge
                E[z + REACH, rows + 8:rows + 16, :] = edge
            CL[z, 0, :, :] = edge
            CL[z, 1, :, :] = edge
            return 0

        lax.fori_loop(0, depth, clear, 0)
        for cond, at in ((has_s_lo, 0), (has_s_hi, depth + REACH)):

            @pl.when(jnp.logical_not(cond))
            def _(at=at):
                for i in range(REACH):
                    for E in (E0, E1):
                        E[at + i, 8:8 + rows, :] = jnp.zeros((rows, nx), F32)
                    for U in (U0, U1):
                        U[at + i] = jnp.zeros((own, nx), F32)

        for side, cp, cb in ((0, has_p_lo, has_b_lo), (1, has_p_hi, has_b_hi)):
            for R, cond in ((UH, cp), (DH, cb)):

                @pl.when(jnp.logical_not(cond))
                def _(R=R, side=side):
                    def zero(z, _):
                        for step in range(2):
                            R[step, side, z] = jnp.zeros((own, nx), F32)
                        return 0

                    lax.fori_loop(0, depth, zero, 0)

    def along_x(D):
        hi = D.astype(jnp.bfloat16)
        lo = (D - hi.astype(F32)).astype(jnp.bfloat16)
        X = jnp.dot(hi, B[...], preferred_element_type=F32)
        X = X + jnp.dot(lo, B[...], preferred_element_type=F32)
        return X * (1.0 / SCALE)

    def incident(step, U, older, into):
        def build(z, _):
            YE[z, 4:8, :] = UH[step, 0, z]
            YE[z, 8:12, :] = U[z + REACH]
            YE[z, 12:16, :] = UH[step, 1, z]
            return 0

        lax.fori_loop(0, depth, build, 0)
        XS[...] = along_x(YE[:, 8:16, :].reshape(depth * 8, nx)).reshape(depth, 8, nx)

        def point(z, _):
            c = U[z + REACH]
            acc = XS[z, 0:4, :] + (3.0 * coefficients[0]) * c
            for j in range(1, 5):
                acc = acc + coefficients[j] * (U[z + REACH - j] + U[z + REACH + j])
            for j in range(1, 5):
                acc = acc + coefficients[j] * (YE[z, 8 - j:12 - j, :] + YE[z, 8 + j:12 + j, :])
            G[1 + step, p, z] = acc
            into(z, 2.0 * c - older(z) + G[0, p, z] * acc + FO[step, z])
            return 0

        lax.fori_loop(0, depth, point, 0)

    def laplace(E, part, parts):
        first, end = part * depth // parts, (part + 1) * depth // parts

        def wide(c, _):
            z0 = c * 8
            D = E[pl.ds(z0 + REACH, 8), 8:8 + rows, :].reshape(8 * rows, nx)
            L[pl.ds(z0, 8)] = along_x(D).reshape(8, rows, nx)
            return 0

        lax.fori_loop(first // 8, end // 8, wide, 0)

        def point(z, _):
            acc = L[z] + (3.0 * coefficients[0]) * E[z + REACH, 8:8 + rows, :]
            for j in range(1, 5):
                acc = acc + coefficients[j] * (E[z + REACH - j, 8:8 + rows, :] + E[z + REACH + j, 8:8 + rows, :])
            for j in range(1, 5):
                acc = acc + coefficients[j] * (
                    E[z + REACH, 8 - j:8 - j + rows, :] + E[z + REACH, 8 + j:8 + j + rows, :]
                )
            L[z] = acc
            return 0

        lax.fori_loop(first, end, point, 0)

    def update(step, q, newer, older, into):
        gather_wait(0, q) if step == 0 else None
        gather_wait(1 + step, q)
        side = 0 if q == 0 else 1 if q == GROUP - 1 else None
        if side is not None:
            wait_rim(step, side)
        at = q * own

        def point(z, _):
            lap = L[z, at:at + own, :]
            if side == 0:
                CL[z, 0, 0:4, :] = DH[step, 0, z]
                for j in range(1, 5):
                    lap = lap + coefficients[j] * CL[z, 0, 4 - j:8 - j, :]
            if side == 1:
                CL[z, 1, 4:8, :] = DH[step, 1, z]
                for j in range(1, 5):
                    lap = lap + coefficients[j] * CL[z, 1, j:j + 4, :]
            value = (
                2.0 * newer(z, at) - older(z, at)
                + G[0, q, z] * (lap + 2.0 * PT[z, at:at + own, :] * G[1 + step, q, z])
            )
            into(z, at, value)
            if step == 0 and side is not None:
                SB[1, side, z] = value
            return 0

        lax.fori_loop(0, depth, point, 0, unroll=4)

    def into_u1(z, v):
        U1[z + REACH] = v

    def into_out(z, v):
        inc_out[z] = v

    def into_e1(z, at, v):
        E1[z + REACH, 8 + at:8 + at + own, :] = v

    def into_probe(z, at, v):
        probe_out[z, at:at + own, :] = v

    def from_e(E):
        return lambda z, at: E[z + REACH, 8 + at:8 + at + own, :]

    def incident_0():
        for i in (0, 1, 3, 4):
            loads[i].wait()
        wait_incident(0, U0)
        incident(0, U0, lambda z: IP[z], into_u1)

    def incident_1():
        wait_incident(1, U1)
        incident(1, U1, lambda z: U0[z + REACH], into_out)

    def update_0(q):
        update(0, q, from_e(E0), lambda z, at: PP[z, at:at + own, :], into_e1)

    def update_1(q):
        update(1, q, from_e(E1), from_e(E0), into_probe)

    low, high = pl.ds(REACH, REACH), pl.ds(depth, REACH)
    tasks = {
        "rims_u0": lambda: rims_incident(0, inow, U0),
        "rims_u1": lambda: rims_incident(1, U1.at[pl.ds(REACH, depth)], U1),
        "pass_u0": lambda: pass_incident(0),
        "pass_u1": lambda: pass_incident(1),
        "own_s": lambda: gather_own(0, stiff),
        "own_s_away": lambda: gather_own(0, stiff, "away"),
        "own_s_along": lambda: gather_own(0, stiff, "along"),
        "own_0_away": lambda: gather_own(1, G.at[1, p], "away"),
        "own_0_along": lambda: gather_own(1, G.at[1, p], "along"),
        "own_0": lambda: gather_own(1, G.at[1, p]),
        "own_1": lambda: gather_own(2, G.at[2, p]),
        "depth_0": lambda: send_depth(0, pnow.at[pl.ds(0, REACH)], pnow.at[pl.ds(depth - REACH, REACH)], E0),
        "depth_1": lambda: send_depth(1, E1.at[low, pl.ds(8, rows)], E1.at[high, pl.ds(8, rows)], E1),
        "pack": pack,
        "constants": constants,
        "rims_0": lambda: (send_rim(0, 0), send_rim(0, 1)),
        "rims_1": lambda: (send_rim(1, 0), send_rim(1, 1)),
        "pass_0": lambda: pass_rim(0),
        "pass_1": lambda: pass_rim(1),
        "incident_0": incident_0,
        "incident_1": incident_1,
        "hear_0": lambda: wait_depth(0, E0),
        "hear_1": lambda: wait_depth(1, E1),
        "loads": lambda: (loads[5].wait(), loads[6].wait()),
    }
    outer = jnp.logical_not(inner)
    for k in range(3):
        for a, name in enumerate("s01"):
            tasks["fwd_%s%d" % (name, k)] = functools.partial(forward, a, k)
            tasks["fwd_%s%d_inner" % (name, k)] = functools.partial(forward, a, k, inner)
            tasks["fwd_%s%d_outer" % (name, k)] = functools.partial(forward, a, k, outer)
    for step in range(2):
        tasks["rims_%d_inner" % step] = lambda step=step: (send_rim(step, 0, inner), send_rim(step, 1, inner))
        tasks["rims_%d_outer" % step] = lambda step=step: (send_rim(step, 0, outer), send_rim(step, 1, outer))
    for part in range(2):
        tasks["lap_0%d" % part] = functools.partial(laplace, E0, part, 2)
        tasks["lap_1%d" % part] = functools.partial(laplace, E1, part, 2)
    for q in range(GROUP):
        tasks["new_0%d" % q] = functools.partial(update_0, q)
        tasks["new_1%d" % q] = functools.partial(update_1, q)
    for name in ORDER:
        tasks[name]()

    for cond, d in pending:
        if cond is None:
            d.wait_send()
        else:
            pl.when(cond)(d.wait_send)


def local(n_probe, n_slab, iprev, inow, forcing, stiff, pprev, pnow, pert):
    depth, own, nx = inow.shape
    rows = pnow.shape[1]
    dma = pltpu.SemaphoreType.DMA
    vm = pltpu.VMEM
    return fresh(*pl.pallas_call(
        functools.partial(kernel, depth, rows, nx, n_probe, n_slab),
        out_shape=(pltpu.VMEM(pnow.shape, F32), pltpu.VMEM(inow.shape, F32)),
        in_specs=[pl.BlockSpec(memory_space=pltpu.HBM)] * 7,
        out_specs=(pl.BlockSpec(memory_space=pltpu.VMEM), pl.BlockSpec(memory_space=pltpu.VMEM)),
        scratch_shapes=[
            vm((depth + 8, own, nx), F32),
            vm((depth + 8, own, nx), F32),
            vm((2, 2, depth, own, nx), F32),
            vm((depth, own, nx), F32),
            vm((2, depth, own, nx), F32),
            vm((depth, 16, nx), F32),
            vm((depth, 8, nx), F32),
            vm((3, GROUP, depth, own, nx), F32),
            vm((depth + 8, rows + 16, nx), F32),
            vm((depth + 8, rows + 16, nx), F32),
            vm((depth, rows, nx), F32),
            vm((depth, rows, nx), F32),
            vm((depth, rows, nx), F32),
            vm((2, 2, depth, own, nx), F32),
            vm((2, 2, depth, own, nx), F32),
            vm((2, depth // 2, own, nx), F32),
            vm((depth, 2, 8, nx), F32),
            vm((nx, nx), jnp.bfloat16),
            dma((3, 8)), dma((3, 8)), dma((2, 6)), dma((2, 4, 2)), dma((2, 4, 3)), dma((2, 4, 2)), dma((7,)),
        ],
        compiler_params=pltpu.CompilerParams(
            collective_id=0, has_side_effects=True, vmem_limit_bytes=48 * 1024 * 1024
        ),
        name="born",
    )(*(pltpu.with_memory_space_constraint(v, pltpu.HBM) for v in (iprev, inow, forcing, stiff, pprev, pnow, pert))))


def hand_over(a, b, a_out, b_out, sems):
    moves = [pltpu.make_async_copy(a, a_out, sems.at[0]), pltpu.make_async_copy(b, b_out, sems.at[1])]
    for m in moves:
        m.start()
    for m in moves:
        m.wait()


def fresh(a, b):
    vmem, any_ = pl.BlockSpec(memory_space=pltpu.VMEM), pl.BlockSpec(memory_space=pl.ANY)
    return pl.pallas_call(
        hand_over,
        out_shape=(jax.ShapeDtypeStruct(a.shape, F32), jax.ShapeDtypeStruct(b.shape, F32)),
        in_specs=[vmem, vmem], out_specs=(any_, any_), name="fresh",
        scratch_shapes=[pltpu.SemaphoreType.DMA((2,))],
    )(pltpu.with_memory_space_constraint(a, pltpu.VMEM), pltpu.with_memory_space_constraint(b, pltpu.VMEM))


def solution(mesh):
    spec = P("slab", "probe", None)
    return jax.shard_map(
        functools.partial(local, mesh.shape["probe"], mesh.shape["slab"]),
        mesh=mesh,
        in_specs=(spec, spec, P(None, "slab", "probe", None), spec, spec, spec, spec),
        out_specs=(spec, spec),
        check_vma=False,
    )
```

```python
import functools

import jax
import jax.numpy as jnp
from jax import lax
from jax.experimental import pallas as pl
from jax.experimental.pallas import tpu as pltpu
from jax.sharding import PartitionSpec as P

coefficients = (-205.0 / 72.0, 8.0 / 5.0, -1.0 / 5.0, 8.0 / 315.0, -1.0 / 560.0)
SCALE = 5040
BAND = (0.0, 8064.0, -1008.0, 128.0, -9.0)

GROUP = 8
REACH = 4
MESH = pl.DeviceIdType.MESH
RELAYED = (True, False)
ORDER = (
    "rims_u0", "own_s_away", "depth_0", "pack", "constants", "pass_u0", "own_s_along", "incident_0", "rims_u1", "own_0", "fwd_s0", "fwd_s1", "fwd_s2", "hear_0", "fwd_00_inner", "fwd_01_inner", "rims_0", "incident_1", "own_1", "lap_00", "lap_01", "pass_0", "fwd_00_outer", "fwd_01_outer", "fwd_02", "loads", "new_00", "new_07", "new_01", "new_02", "new_03", "new_04", "new_05", "new_06", "depth_1", "fwd_10", "fwd_11", "rims_1", "hear_1", "lap_10", "lap_11", "fwd_12", "pass_1", "new_11", "new_12", "new_13", "new_14", "new_15", "new_16", "new_10", "new_17",
)
F32 = jnp.float32


def kernel(
    depth, rows, nx, n_probe, n_slab,
    iprev, inow, forcing, stiff, pprev, pnow, pert,
    probe_out, inc_out,
    U0, U1, UH, IP, FO, YE, XS, G, E0, E1, PP, PT, L, SB, DH, RX, CL, B,
    ssG, rsG, ssU, rsU, ssD, rsD, ls,
):
    Pi = lax.axis_index("probe")
    Si = lax.axis_index("slab")
    p = Pi % GROUP
    zl = p // 2
    yl = p % 2
    z1 = zl + 1 - 2 * (zl % 2)
    z2 = (zl + 2) % 4
    z3 = 3 - zl
    base = Pi - p
    inner = jnp.logical_or(zl == 1, zl == 2)
    partner = Pi + 1 - 2 * yl
    own = rows // GROUP

    def zdev(k):
        return (base + (z1, z2, z3)[k] * 2 + yl, Si)

    def zslot(k):
        return (z1, z2, z3)[k] * 2 + yl

    has_p_lo, has_p_hi = Pi > 0, Pi < n_probe - 1
    has_b_lo, has_b_hi = Pi >= GROUP, Pi < n_probe - GROUP
    has_s_lo, has_s_hi = Si > 0, Si < n_slab - 1
    block, last = Pi // GROUP, n_probe // GROUP - 1
    from_lo, relay_lo, to_lo = block == 2, block == 0, block == 1
    from_hi, relay_hi, to_hi = block == last - 2, block == last, block == last - 1

    loads = [
        pltpu.make_async_copy(inow, U0.at[pl.ds(REACH, depth)], ls.at[0]),
        pltpu.make_async_copy(stiff, G.at[0, p], ls.at[1]),
        pltpu.make_async_copy(pnow, E0.at[pl.ds(REACH, depth), pl.ds(8, rows)], ls.at[2]),
        pltpu.make_async_copy(iprev, IP, ls.at[3]),
        pltpu.make_async_copy(forcing, FO, ls.at[4]),
        pltpu.make_async_copy(pprev, PP, ls.at[5]),
        pltpu.make_async_copy(pert, PT, ls.at[6]),
    ]
    for c in loads:
        c.start()

    bar = pltpu.get_barrier_semaphore()

    def hello(dev):
        pl.semaphore_signal(bar, inc=1, device_id=dev, device_id_type=MESH)

    for k in range(3):
        hello(zdev(k))
    hello((partner, Si))
    sides = [
        (has_p_lo, (Pi - 1, Si)), (has_p_hi, (Pi + 1, Si)),
        (has_b_lo, (Pi - GROUP, Si)), (has_b_hi, (Pi + GROUP, Si)),
        (has_s_lo, (Pi, Si - 1)), (has_s_hi, (Pi, Si + 1)),
        (Pi > 1, (Pi - 2, Si)), (Pi < n_probe - 2, (Pi + 2, Si)),
        (jnp.logical_or(from_lo, relay_hi), (Pi - 2 * GROUP, Si)),
        (jnp.logical_or(from_hi, relay_lo), (Pi + 2 * GROUP, Si)),
    ]
    for cond, dev in sides:
        pl.when(cond)(functools.partial(hello, dev))
    peers = 4
    for cond, _ in sides:
        peers = peers + cond.astype(jnp.int32)
    pl.semaphore_wait(bar, peers)

    def remote(src, dst, ssem, rsem, dev):
        return pltpu.make_async_remote_copy(
            src_ref=src, dst_ref=dst, send_sem=ssem, recv_sem=rsem,
            device_id=dev, device_id_type=MESH,
        )

    pending = []

    def send(cond, desc):
        if cond is None:
            desc.start()
        else:
            pl.when(cond)(desc.start)
        pending.append((cond, desc))

    half = depth // 2
    near, far = pl.ds(0, half), pl.ds(half, half)
    lower, upper = yl == 0, yl == 1

    def rims_incident(step, src, U):
        def to(cond, dev, side, part, k):
            send(cond, remote(src.at[part], UH.at[step, side, part], ssU.at[step, k], rsU.at[step, side, k % 2], dev))

        for part, k in ((near, 0), (far, 1)):
            to(lower, (partner, Si), 0, part, k)
            to(upper, (partner, Si), 1, part, k)
        send(has_s_lo, remote(src.at[pl.ds(0, REACH)], U.at[pl.ds(depth + REACH, REACH)],
                              ssU.at[step, 4], rsU.at[step, 3, 0], (Pi, Si - 1)))
        send(has_s_hi, remote(src.at[pl.ds(depth - REACH, REACH)], U.at[pl.ds(0, REACH)],
                              ssU.at[step, 5], rsU.at[step, 2, 0], (Pi, Si + 1)))
        for part, k in () if RELAYED[step] else ((near, 2), (far, 3)):
            to(jnp.logical_and(lower, has_p_lo), (Pi - 1, Si), 1, part, k)
            to(jnp.logical_and(upper, has_p_hi), (Pi + 1, Si), 0, part, k)

    def arrived(step, side, k):
        r = UH.at[step, side, (near, far)[k]]
        remote(r, r, ssU.at[step, 3], rsU.at[step, side, k], (partner, Si)).wait_recv()

    def pass_incident(step):
        for mine, there, side, dev in (
            (lower, Pi < n_probe - 2, 1, (Pi + 2, Si)),
            (upper, Pi > 1, 0, (Pi - 2, Si)),
        ):
            for part, k in ((near, 0), (far, 1)):
                pl.when(mine)(functools.partial(arrived, step, side, k))
                send(jnp.logical_and(mine, there),
                     remote(UH.at[step, side, part], UH.at[step, 1 - side, part], ssU.at[step, 2 + k],
                            rsU.at[step, 1 - side, k], dev))

    def wait_incident(step, U):
        for mine, side, there in ((lower, 1, has_p_lo), (upper, 0, has_p_hi)):

            @pl.when(mine)
            def _(side=side):
                if not RELAYED[step]:
                    arrived(step, side, 0)
                    arrived(step, side, 1)

            @pl.when(jnp.logical_and(mine, there))
            def _(side=side):
                arrived(step, 1 - side, 0)
                arrived(step, 1 - side, 1)

        for side, cond, at in ((2, has_s_lo, 0), (3, has_s_hi, depth + REACH)):
            r = U.at[pl.ds(at, REACH)]
            d = remote(r, r, ssU.at[step, 3], rsU.at[step, side, 0], (partner, Si))
            pl.when(cond)(d.wait_recv)

    def send_depth(step, low, high, E):
        send(has_s_lo, remote(low, E.at[pl.ds(depth + REACH, REACH), pl.ds(8, rows)],
                              ssD.at[step, 2, 0], rsD.at[step, 3, 0], (Pi, Si - 1)))
        send(has_s_hi, remote(high, E.at[pl.ds(0, REACH), pl.ds(8, rows)],
                              ssD.at[step, 3, 0], rsD.at[step, 2, 0], (Pi, Si + 1)))

    def wait_depth(step, E):
        for side, cond, at in ((2, has_s_lo, 0), (3, has_s_hi, depth + REACH)):
            r = E.at[pl.ds(at, REACH), pl.ds(8, rows)]
            d = remote(r, r, ssD.at[step, side, 0], rsD.at[step, side, 0], (partner, Si))
            pl.when(cond)(d.wait_recv)

    def send_rim(step, side, role=None):
        cond, by_x, shift, hop = (
            (has_b_lo, from_lo, -GROUP, -2 * GROUP), (has_b_hi, from_hi, GROUP, 2 * GROUP)
        )[side]
        if role is not None:
            cond, by_x = jnp.logical_and(cond, role), jnp.logical_and(by_x, role)

        def to(cond, dst, part, k, rsem, dev):
            send(cond, remote(SB.at[step, side, part], dst, ssD.at[step, side, k], rsem, dev))

        out = DH.at[step, 1 - side]
        to(cond, out.at[near], near, 0, rsD.at[step, 1 - side, 0], (Pi + shift, Si))
        to(jnp.logical_and(cond, jnp.logical_not(by_x)), out.at[far], far, 1,
           rsD.at[step, 1 - side, 1], (Pi + shift, Si))
        to(by_x, RX.at[step], far, 2, rsD.at[step, 2, 1], (Pi + hop, Si))

    def pass_rim(step):
        for cond, side, shift in ((relay_lo, 1, GROUP), (relay_hi, 0, -GROUP)):

            @pl.when(cond)
            def _():
                remote(RX.at[step], RX.at[step], ssD.at[step, 3, 1], rsD.at[step, 2, 1], (partner, Si)).wait_recv()

            send(cond, remote(RX.at[step], DH.at[step, side, far], ssD.at[step, 2, 1], rsD.at[step, side, 1],
                              (Pi + shift, Si)))

    def wait_rim(step, side):
        for part, k in ((near, 0), (far, 1)):
            r = DH.at[step, side, part]
            d = remote(r, r, ssD.at[step, side, k], rsD.at[step, side, k], (partner, Si))
            pl.when((has_b_lo, has_b_hi)[side])(d.wait_recv)

    def gather_own(a, src, part="all"):
        dst = G.at[a, p]
        for k, up, there in ((0, zl % 2 == 0, None), (1, zl < 2, None), (2, zl == 1, inner)):
            if part != "all":
                way = (up == upper) if part == "away" else (up != upper)
                there = way if there is None else jnp.logical_and(there, way)
            send(there, remote(src, dst, ssG.at[a, 1 + k], rsG.at[a, p], zdev(k)))
        if part != "along":
            send(None, remote(src, dst, ssG.at[a, 0], rsG.at[a, p], (partner, Si)))

    def forward(a, k, role=None):
        slot = zslot(k)
        r = G.at[a, slot]
        arrival = remote(r, r, ssG.at[a, 4 + k], rsG.at[a, slot], (partner, Si))
        if role is None:
            arrival.wait_recv()
        else:
            pl.when(role)(arrival.wait_recv)
        if k == 1:
            relay = inner if role is None else jnp.logical_and(inner, role)
            send(relay, remote(r, r, ssG.at[a, 7], rsG.at[a, slot], zdev(0)))
        send(role, remote(r, r, ssG.at[a, 4 + k], rsG.at[a, slot], (partner, Si)))

    def gather_wait(a, q):
        r = G.at[a, q]
        d = remote(r, r, ssG.at[a, 0], rsG.at[a, q], (partner, Si))
        pl.when((q % 2) != yl)(d.wait_recv)

    def pack():
        loads[2].wait()

        def row(z, _):
            SB[0, 0, z] = E0[z + REACH, 8:12, :]
            SB[0, 1, z] = E0[z + REACH, rows + 4:rows + 8, :]
            return 0

        lax.fori_loop(0, depth, row, 0)

    def constants():
        def band(i, _):
            r = lax.broadcasted_iota(jnp.int32, (64, nx), 0) + i * 64
            c = lax.broadcasted_iota(jnp.int32, (64, nx), 1)
            gap = jnp.abs(r - c)
            v = jnp.zeros((64, nx), F32)
            for j in range(1, 5):
                v = jnp.where(gap == j, BAND[j], v)
            B[pl.ds(pl.multiple_of(i * 64, 64), 64), :] = v.astype(jnp.bfloat16)
            return 0

        lax.fori_loop(0, nx // 64, band, 0)

        edge = jnp.zeros((8, nx), F32)

        def clear(z, _):
            for E in (E0, E1):
                E[z + REACH, 0:8, :] = edge
                E[z + REACH, rows + 8:rows + 16, :] = edge
            CL[z, 0, :, :] = edge
            CL[z, 1, :, :] = edge
            return 0

        lax.fori_loop(0, depth, clear, 0)
        for cond, at in ((has_s_lo, 0), (has_s_hi, depth + REACH)):

            @pl.when(jnp.logical_not(cond))
            def _(at=at):
                for i in range(REACH):
                    for E in (E0, E1):
                        E[at + i, 8:8 + rows, :] = jnp.zeros((rows, nx), F32)
                    for U in (U0, U1):
                        U[at + i] = jnp.zeros((own, nx), F32)

        for side, cp, cb in ((0, has_p_lo, has_b_lo), (1, has_p_hi, has_b_hi)):
            for R, cond in ((UH, cp), (DH, cb)):

                @pl.when(jnp.logical_not(cond))
                def _(R=R, side=side):
                    def zero(z, _):
                        for step in range(2):
                            R[step, side, z] = jnp.zeros((own, nx), F32)
                        return 0

                    lax.fori_loop(0, depth, zero, 0)

    def along_x(D):
        hi = D.astype(jnp.bfloat16)
        lo = (D - hi.astype(F32)).astype(jnp.bfloat16)
        X = jnp.dot(hi, B[...], preferred_element_type=F32)
        X = X + jnp.dot(lo, B[...], preferred_element_type=F32)
        return X * (1.0 / SCALE)

    def incident(step, U, older, into):
        def build(z, _):
            YE[z, 4:8, :] = UH[step, 0, z]
            YE[z, 8:12, :] = U[z + REACH]
            YE[z, 12:16, :] = UH[step, 1, z]
            return 0

        lax.fori_loop(0, depth, build, 0)
        XS[...] = along_x(YE[:, 8:16, :].reshape(depth * 8, nx)).reshape(depth, 8, nx)

        def point(z, _):
            c = U[z + REACH]
            acc = XS[z, 0:4, :] + (3.0 * coefficients[0]) * c
            for j in range(1, 5):
                acc = acc + coefficients[j] * (U[z + REACH - j] + U[z + REACH + j])
            for j in range(1, 5):
                acc = acc + coefficients[j] * (YE[z, 8 - j:12 - j, :] + YE[z, 8 + j:12 + j, :])
            G[1 + step, p, z] = acc
            into(z, 2.0 * c - older(z) + G[0, p, z] * acc + FO[step, z])
            return 0

        lax.fori_loop(0, depth, point, 0)

    def laplace(E, part, parts):
        first, end = part * depth // parts, (part + 1) * depth // parts

        def wide(c, _):
            z0 = c * 8
            D = E[pl.ds(z0 + REACH, 8), 8:8 + rows, :].reshape(8 * rows, nx)
            L[pl.ds(z0, 8)] = along_x(D).reshape(8, rows, nx)
            return 0

        lax.fori_loop(first // 8, end // 8, wide, 0)

        def point(z, _):
            acc = L[z] + (3.0 * coefficients[0]) * E[z + REACH, 8:8 + rows, :]
            for j in range(1, 5):
                acc = acc + coefficients[j] * (E[z + REACH - j, 8:8 + rows, :] + E[z + REACH + j, 8:8 + rows, :])
            for j in range(1, 5):
                acc = acc + coefficients[j] * (
                    E[z + REACH, 8 - j:8 - j + rows, :] + E[z + REACH, 8 + j:8 + j + rows, :]
                )
            L[z] = acc
            return 0

        lax.fori_loop(first, end, point, 0)

    def update(step, q, newer, older, into):
        gather_wait(0, q) if step == 0 else None
        gather_wait(1 + step, q)
        side = 0 if q == 0 else 1 if q == GROUP - 1 else None
        if side is not None:
            wait_rim(step, side)
        at = q * own

        def point(z, _):
            lap = L[z, at:at + own, :]
            if side == 0:
                CL[z, 0, 0:4, :] = DH[step, 0, z]
                for j in range(1, 5):
                    lap = lap + coefficients[j] * CL[z, 0, 4 - j:8 - j, :]
            if side == 1:
                CL[z, 1, 4:8, :] = DH[step, 1, z]
                for j in range(1, 5):
                    lap = lap + coefficients[j] * CL[z, 1, j:j + 4, :]
            value = (
                2.0 * newer(z, at) - older(z, at)
                + G[0, q, z] * (lap + 2.0 * PT[z, at:at + own, :] * G[1 + step, q, z])
            )
            into(z, at, value)
            if step == 0 and side is not None:
                SB[1, side, z] = value
            return 0

        lax.fori_loop(0, depth, point, 0, unroll=4)

    def into_u1(z, v):
        U1[z + REACH] = v

    def into_out(z, v):
        inc_out[z] = v

    def into_e1(z, at, v):
        E1[z + REACH, 8 + at:8 + at + own, :] = v

    def into_probe(z, at, v):
        probe_out[z, at:at + own, :] = v

    def from_e(E):
        return lambda z, at: E[z + REACH, 8 + at:8 + at + own, :]

    def incident_0():
        for i in (0, 1, 3, 4):
            loads[i].wait()
        wait_incident(0, U0)
        incident(0, U0, lambda z: IP[z], into_u1)

    def incident_1():
        wait_incident(1, U1)
        incident(1, U1, lambda z: U0[z + REACH], into_out)

    def update_0(q):
        update(0, q, from_e(E0), lambda z, at: PP[z, at:at + own, :], into_e1)

    def update_1(q):
        update(1, q, from_e(E1), from_e(E0), into_probe)

    low, high = pl.ds(REACH, REACH), pl.ds(depth, REACH)
    tasks = {
        "rims_u0": lambda: rims_incident(0, inow, U0),
        "rims_u1": lambda: rims_incident(1, U1.at[pl.ds(REACH, depth)], U1),
        "pass_u0": lambda: pass_incident(0),
        "pass_u1": lambda: pass_incident(1),
        "own_s": lambda: gather_own(0, stiff),
        "own_s_away": lambda: gather_own(0, stiff, "away"),
        "own_s_along": lambda: gather_own(0, stiff, "along"),
        "own_0_away": lambda: gather_own(1, G.at[1, p], "away"),
        "own_0_along": lambda: gather_own(1, G.at[1, p], "along"),
        "own_0": lambda: gather_own(1, G.at[1, p]),
        "own_1": lambda: gather_own(2, G.at[2, p]),
        "depth_0": lambda: send_depth(0, pnow.at[pl.ds(0, REACH)], pnow.at[pl.ds(depth - REACH, REACH)], E0),
        "depth_1": lambda: send_depth(1, E1.at[low, pl.ds(8, rows)], E1.at[high, pl.ds(8, rows)], E1),
        "pack": pack,
        "constants": constants,
        "rims_0": lambda: (send_rim(0, 0), send_rim(0, 1)),
        "rims_1": lambda: (send_rim(1, 0), send_rim(1, 1)),
        "pass_0": lambda: pass_rim(0),
        "pass_1": lambda: pass_rim(1),
        "incident_0": incident_0,
        "incident_1": incident_1,
        "hear_0": lambda: wait_depth(0, E0),
        "hear_1": lambda: wait_depth(1, E1),
        "loads": lambda: (loads[5].wait(), loads[6].wait()),
    }
    outer = jnp.logical_not(inner)
    for k in range(3):
        for a, name in enumerate("s01"):
            tasks["fwd_%s%d" % (name, k)] = functools.partial(forward, a, k)
            tasks["fwd_%s%d_inner" % (name, k)] = functools.partial(forward, a, k, inner)
            tasks["fwd_%s%d_outer" % (name, k)] = functools.partial(forward, a, k, outer)
    for step in range(2):
        tasks["rims_%d_inner" % step] = lambda step=step: (send_rim(step, 0, inner), send_rim(step, 1, inner))
        tasks["rims_%d_outer" % step] = lambda step=step: (send_rim(step, 0, outer), send_rim(step, 1, outer))
    for part in range(2):
        tasks["lap_0%d" % part] = functools.partial(laplace, E0, part, 2)
        tasks["lap_1%d" % part] = functools.partial(laplace, E1, part, 2)
    for q in range(GROUP):
        tasks["new_0%d" % q] = functools.partial(update_0, q)
        tasks["new_1%d" % q] = functools.partial(update_1, q)
    for name in ORDER:
        tasks[name]()

    for cond, d in pending:
        if cond is None:
            d.wait_send()
        else:
            pl.when(cond)(d.wait_send)


def local(n_probe, n_slab, iprev, inow, forcing, stiff, pprev, pnow, pert):
    depth, own, nx = inow.shape
    rows = pnow.shape[1]
    dma = pltpu.SemaphoreType.DMA
    vm = pltpu.VMEM
    return fresh(*pl.pallas_call(
        functools.partial(kernel, depth, rows, nx, n_probe, n_slab),
        out_shape=(pltpu.VMEM(pnow.shape, F32), pltpu.VMEM(inow.shape, F32)),
        in_specs=[pl.BlockSpec(memory_space=pltpu.HBM)] * 7,
        out_specs=(pl.BlockSpec(memory_space=pltpu.VMEM), pl.BlockSpec(memory_space=pltpu.VMEM)),
        scratch_shapes=[
            vm((depth + 8, own, nx), F32),
            vm((depth + 8, own, nx), F32),
            vm((2, 2, depth, own, nx), F32),
            vm((depth, own, nx), F32),
            vm((2, depth, own, nx), F32),
            vm((depth, 16, nx), F32),
            vm((depth, 8, nx), F32),
            vm((3, GROUP, depth, own, nx), F32),
            vm((depth + 8, rows + 16, nx), F32),
            vm((depth + 8, rows + 16, nx), F32),
            vm((depth, rows, nx), F32),
            vm((depth, rows, nx), F32),
            vm((depth, rows, nx), F32),
            vm((2, 2, depth, own, nx), F32),
            vm((2, 2, depth, own, nx), F32),
            vm((2, depth // 2, own, nx), F32),
            vm((depth, 2, 8, nx), F32),
            vm((nx, nx), jnp.bfloat16),
            dma((3, 8)), dma((3, 8)), dma((2, 6)), dma((2, 4, 2)), dma((2, 4, 3)), dma((2, 4, 2)), dma((7,)),
        ],
        compiler_params=pltpu.CompilerParams(
            collective_id=0, has_side_effects=True, vmem_limit_bytes=48 * 1024 * 1024
        ),
        name="born",
    )(*(pltpu.with_memory_space_constraint(v, pltpu.HBM) for v in (iprev, inow, forcing, stiff, pprev, pnow, pert))))


def hand_over(a, b, a_out, b_out, sems):
    moves = [pltpu.make_async_copy(a, a_out, sems.at[0]), pltpu.make_async_copy(b, b_out, sems.at[1])]
    for m in moves:
        m.start()
    for m in moves:
        m.wait()


def fresh(a, b):
    vmem, any_ = pl.BlockSpec(memory_space=pltpu.VMEM), pl.BlockSpec(memory_space=pl.ANY)
    return pl.pallas_call(
        hand_over,
        out_shape=(jax.ShapeDtypeStruct(a.shape, F32), jax.ShapeDtypeStruct(b.shape, F32)),
        in_specs=[vmem, vmem], out_specs=(any_, any_), name="fresh",
        scratch_shapes=[pltpu.SemaphoreType.DMA((2,))],
    )(pltpu.with_memory_space_constraint(a, pltpu.VMEM), pltpu.with_memory_space_constraint(b, pltpu.VMEM))


def solution(mesh):
    spec = P("slab", "probe", None)
    return jax.shard_map(
        functools.partial(local, mesh.shape["probe"], mesh.shape["slab"]),
        mesh=mesh,
        in_specs=(spec, spec, P(None, "slab", "probe", None), spec, spec, spec, spec),
        out_specs=(spec, spec),
        check_vma=False,
    )
```
